32 devices in a mesh: dp: 16 (over z, y, x), pipe: 2 (over core).
Axes of the slice: x: 2, y: 2, z: 4, core: 2. Of those that a mesh axis runs over, the one named last changes fastest.
Arguments:
- blocks: bfloat16 [2, 3072, 1024], P(None, 'dp'), may hold values from -6 to 6
- dest: int32 [2, 16, 48], replicated, may hold values from 0 to 15, as said below
- resets: int32 [2, 32], replicated, may hold values from 1 to 3071
- w_query: bfloat16 [4, 1024, 512], P('pipe'), may hold values from -0.1875 to 0.1875
- gain: float32 [4, 1024], P('pipe'), may hold values from 0.5 to 1.5
- decay: float32 [4, 8], P('pipe'), may hold values from 0 to 1
- cot: bfloat16 [2, 3072, 1024], P(None, 'dp'), may hold values from -0.076171875 to 0.076171875
Outputs:
- weight_grads: float32 [4, 1024, 512], P('pipe', 'dp')
The draws below stay inside these ranges and needn't reach their ends.
Inputs may be any that keep to these rules, and one draw needn't show every extreme that they name: dest[m, i, j] = (i + o) mod 16 for an offset o that depends only on m and j, so each rank receives exactly one block j for every j; a rank sends at most 3 of its blocks to one rank, and exactly 3 to some rank.
All inputs are finite; a program needn't handle non-finite values.
Results may differ from the reference program's by a relative error of at most 0.018.
Values may be sent and summed in bfloat16 or wider, within the bound.
A program may use at most 64 MiB of HBM per device.

```python
import jax
import jax.numpy as jnp
from jax import lax

D = 1024
H = 8
DK = 64
DV = 128
MB = 2
ROWS = 192
CH = 4
P_SIZE = 4
NRES = 32
SEQ = 3072
CPD = 48
CAP = 3
N_DP = 16


def draw_dest(key, part):
    keys = jax.random.split(jax.random.fold_in(key, 7), MB)

    def one_batch(batch_key):
        sigma = jax.random.permutation(batch_key, N_DP * CAP)[:CPD]
        offset = (sigma % N_DP).astype(jnp.int32)
        ranks = jnp.arange(N_DP, dtype=jnp.int32)
        return ((ranks[:, None] + offset[None, :]) % N_DP).astype(jnp.int32)
    return jax.vmap(one_batch)(keys).astype(jnp.int32)


def draw_decay(key, part):
    base = jax.random.fold_in(key, 11)
    pick_key, rate_key = jax.random.split(base)
    share = 0.5
    pick = jax.random.uniform(pick_key, (P_SIZE, H), jnp.float32)
    spread = jax.random.uniform(rate_key, (P_SIZE, H), jnp.float32)
    fast_lo = jnp.log(1.0 / 50.0)
    fast_hi = jnp.log(1.0 / 30.0)
    slow_lo = jnp.log(0.25 / ROWS)
    slow_hi = jnp.log(2.0 / ROWS)
    fast = jnp.exp(fast_lo + spread * (fast_hi - fast_lo))
    slow = jnp.exp(slow_lo + spread * (slow_hi - slow_lo))
    rate = jnp.where(pick < share, fast, slow)
    return jnp.exp(-rate).astype(jnp.float32)


def touch_ends(drawn, rng, smallest, high):
    longest = drawn.shape.index(max(drawn.shape))
    spots = []
    for shift in (0, 1):
        where = [jax.random.randint(jax.random.fold_in(rng, axis), (), 0, length) for axis, length in enumerate(drawn.shape)]
        where[longest] = (where[longest] + shift) % drawn.shape[longest]
        spots.append(tuple(where))
    return drawn.at[spots[0]].set(smallest).at[spots[1]].set(high)


def block_levels(key, shape, shards, least, high):
    def one(position, shards_of):
        steps = jax.random.uniform(jax.random.fold_in(jax.random.fold_in(key, 6), position), (shards_of,), jnp.float32, least / len(shards), high / len(shards))
        return jnp.repeat(jnp.exp(steps), shape[position] // shards_of).reshape((-1,) + (1,) * (len(shape) - position - 1))

    level = one(*shards[0])
    for cut in shards[1:]:
        level = level * one(*cut)
    return level


def noise(rng, extent, scale, most, shards=(), kind=jnp.bfloat16):
    array = jax.random.normal(rng, extent, jnp.float32) * scale
    if len(shards) > 0:
        array = block_levels(rng, extent, shards, -0.22, 0.18) * array
    return jnp.clip(array, min=-most, max=most).astype(kind)


def setup_inputs(seed: int = 0) -> dict:
    key_list = jax.random.split(jax.random.key(seed), 8)
    return {
        "blocks": noise(key_list[0], (MB, SEQ, D), 1.0, 6.0, ((1, 16),)),
        "dest": draw_dest(jax.random.fold_in(key_list[7], 71), 0),
        "resets": touch_ends(jax.random.randint(key_list[2], (MB, NRES), 1, SEQ), jax.random.fold_in(key_list[2], 1), 1, SEQ - 1).astype(jnp.int32),
        "w_query": noise(key_list[3], (P_SIZE, D, H * DK), D ** -0.5, 0.1875, ((0, 2),)),
        "gain": jnp.clip(1.0 + 0.1 * jax.random.normal(key_list[4], (P_SIZE, D), jnp.float32), 0.5, 1.5),
        "decay": draw_decay(jax.random.fold_in(key_list[7], 71), 0),
        "cot": noise(key_list[6], (MB, SEQ, D), ((2 * SEQ) ** -0.5), 0.076171875, ((1, 16),)),
    }


EPS = 1e-05

def normed_project(x, weight, gain, extra):
    x32 = x.astype(jnp.float32)
    scale = lax.rsqrt(lax.optimization_barrier(jnp.mean(x32 * x32, axis=-1, keepdims=True)) + EPS)
    z = (x32 * scale * gain).astype(jnp.bfloat16)
    q = (jnp.dot(z, weight, preferred_element_type=jnp.float32) + extra).astype(jnp.bfloat16)
    return (z, q)

def tables(log_rate, flags):
    count = jnp.cumsum(flags)
    index = jnp.arange(flags.shape[0]).astype(jnp.float32)
    diff = index[:, None] - index[None, :]
    same = (count[:, None] == count[None, :]) & (diff >= 0)
    intra = jnp.where(same[None], jnp.exp(diff[None] * log_rate[:, None, None]), 0.0)
    return intra

def finish(x, heads_out):
    normal = heads_out * lax.rsqrt(lax.optimization_barrier(jnp.mean(heads_out * heads_out, axis=-1, keepdims=True)) + EPS)
    return (x.astype(jnp.float32) + normal.reshape(x.shape)).astype(jnp.bfloat16)

def layer(x, weight, gain, log_rate, flags, extra):
    z, q = normed_project(x, weight, gain, extra)
    length = x.shape[0]
    query_rows = q.astype(jnp.float32).reshape(length, H, DK)
    value_rows = z.astype(jnp.float32).reshape(length, H, DV)
    intra = tables(log_rate, flags)
    scores = jnp.einsum('thk,shk->hts', query_rows, query_rows) * intra
    mixing_weights = lax.optimization_barrier(scores.astype(jnp.bfloat16)).astype(jnp.float32)
    outputs = jnp.einsum('hts,shv->thv', mixing_weights, value_rows)
    return (finish(x, outputs), z)

def reference(blocks, dest, resets, w_query, gain, decay, cot):
    pieces = blocks.reshape(MB, N_DP, CPD, CH, D)
    source = jnp.argsort(dest, axis=1).astype(jnp.int32)
    packed = jnp.take_along_axis(pieces, source[:, :, :, None, None], axis=1).reshape(MB, SEQ, D)
    positions = jnp.arange(SEQ).astype(jnp.int32)
    flags = jnp.any(positions[None, :, None] == resets[:, None, :], axis=-1).astype(jnp.float32)
    log_rate = jnp.log(decay)
    windows = jax.checkpoint(jax.vmap(layer, in_axes=(0, None, None, None, 0, 0)))
    grads = jnp.zeros((P_SIZE, D, H * DK), jnp.float32)
    for batch in range(MB):
        flag_rows = flags[batch].reshape(N_DP, ROWS)
        start_rows = packed[batch].reshape(N_DP, ROWS, D)
        target = cot[batch].astype(jnp.float32)

        def total(extras):
            stream = start_rows
            saved = []
            for depth in range(P_SIZE):
                stream, z = windows(stream, w_query[depth], gain[depth], log_rate[depth], flag_rows, extras[depth])
                saved.append(z.reshape(SEQ, D))
            loss = jnp.sum(stream.reshape(SEQ, D).astype(jnp.float32) * target)
            return (loss, jnp.stack(saved))
        extras = jnp.zeros((P_SIZE, N_DP, ROWS, H * DK), jnp.float32)
        loss, pullback, normals = jax.vjp(total, extras, has_aux=True)
        grad_extra, = pullback(jnp.ones((), jnp.float32))
        per_layer = []
        for depth in range(P_SIZE):
            per_layer.append(jnp.dot(normals[depth].astype(jnp.float32).T, grad_extra[depth].reshape(SEQ, H * DK), precision=lax.Precision.HIGHEST, preferred_element_type=jnp.float32))
        grads = grads + jnp.stack(per_layer)
    return grads
```

```python
import functools

import jax
import jax.numpy as jnp
from jax import lax
from jax.experimental import pallas as pl
from jax.experimental.pallas import tpu as pltpu
from jax.sharding import PartitionSpec as P

CH = 4


EPS = 1e-05


def shifted(x, axis, by):
    devices = lax.axis_size(axis)
    pairs = [(i, i + by) for i in range(devices) if 0 <= i + by < devices]
    return lax.ppermute(x, axis, pairs)


def shortened(x):

    def short(part):
        return part.astype(jnp.bfloat16) if part.dtype == jnp.float32 else part

    return jax.tree.map(short, x)


def normed_project(x, weight, gain, extra):
    x32 = x.astype(jnp.float32)
    scale = lax.rsqrt(jnp.mean(x32 * x32, axis=-1, keepdims=True) + EPS)
    z = (x32 * scale * gain).astype(jnp.bfloat16)
    q = (jnp.dot(z, weight, preferred_element_type=jnp.float32) + extra).astype(jnp.bfloat16)
    return (z, q)


def tables(log_rate, flags):
    count = jnp.cumsum(flags)
    index = jnp.arange(flags.shape[0]).astype(jnp.float32)
    diff = index[:, None] - index[None, :]
    same = (count[:, None] == count[None, :]) & (diff >= 0)
    return jnp.where(same[None], jnp.exp(diff[None] * log_rate[:, None, None]), 0.0)


def section_tables(log_rate, flags):
    length = flags.shape[0]
    intra = tables(log_rate.reshape(-1), flags)
    return intra.reshape(log_rate.shape[0], log_rate.shape[1], length, length)


def finish(x, heads_out):
    normal = heads_out * lax.rsqrt(jnp.mean(heads_out * heads_out, axis=-1, keepdims=True) + EPS)
    return (x.astype(jnp.float32) + normal.reshape(x.shape)).astype(jnp.bfloat16)


def local_layer(x, extra, weight, gain_row, intra):
    z, q = normed_project(x, weight, gain_row, extra)
    heads = intra.shape[0]
    length = x.shape[0]
    query_rows = q.astype(jnp.float32).reshape(length, heads, -1)
    value_rows = z.reshape(length, heads, -1)
    scores = jnp.einsum("thk,shk->hts", query_rows, query_rows) * intra
    mixing_weights = scores.astype(jnp.bfloat16)
    outputs = jnp.einsum(
        "hts,shv->thv", mixing_weights, value_rows, preferred_element_type=jnp.float32
    )
    return (finish(x, outputs), z)


def section(x, extras, weight, gain, intra):
    normals = []
    for depth in range(weight.shape[0]):
        x, z = local_layer(x, extras[depth], weight[depth], gain[depth], intra[depth])
        normals.append(z)
    return (x, jnp.stack(normals))


def pipelined(blocks, dest, resets, w_query, gain, decay, cot):
    groups = lax.axis_size("dp")
    segments = lax.axis_size("pipe")
    rank = lax.axis_index("dp")
    segment = lax.axis_index("pipe")
    batches, rows, width = blocks.shape
    per_rank = rows // CH
    room = (per_rank + groups - 1) // groups
    mine = blocks.reshape(batches, per_rank, CH * width)
    own = lax.dynamic_index_in_dim(dest, rank, 1, keepdims=False)
    order = jnp.arange(per_rank)
    before_mask = order[None, :] < order[:, None]
    matching = own[:, :, None] == own[:, None, :]
    before = jnp.sum((matching & before_mask[None]).astype(jnp.int32), axis=2)
    target = own * room + before
    slot_ids = jnp.arange(groups * room, dtype=jnp.int32)
    send_map = (target[:, None, :] == slot_ids[None, :, None]).astype(jnp.bfloat16)
    outgoing = jnp.einsum(
        "mtj,mjc->mtc", send_map, mine, preferred_element_type=jnp.float32
    ).astype(jnp.bfloat16)
    incoming = lax.all_to_all(outgoing, "dp", split_axis=1, concat_axis=1, tiled=True)
    hits = (dest == rank).astype(jnp.int32)
    rank_in = jnp.cumsum(hits, axis=2) - 1
    senders = jnp.arange(groups, dtype=jnp.int32)[None, :, None]
    source = jnp.sum(hits * (senders * room + rank_in), axis=1)
    recv_map = (source[:, :, None] == slot_ids[None, None, :]).astype(jnp.bfloat16)
    packed = (
        jnp.einsum("mjt,mtc->mjc", recv_map, incoming, preferred_element_type=jnp.float32)
        .astype(jnp.bfloat16)
        .reshape(batches, rows, width)
    )
    positions = rank * rows + jnp.arange(rows, dtype=jnp.int32)
    flags = jnp.any(positions[None, :, None] == resets[:, None, :], axis=-1).astype(jnp.float32)
    layers = w_query.shape[0]
    hidden_qk = w_query.shape[2]
    log_rate = jnp.log(decay)
    zero_extra = jnp.zeros((layers, rows, hidden_qk), jnp.float32)
    zero_rows = jnp.zeros((rows, width), jnp.bfloat16)
    ticks = batches + segments - 1

    def forward_tick(tick, carry):
        inbox, saved_x = carry
        batch = tick - segment
        valid = (batch >= 0) & (batch < batches)
        pick = jnp.clip(batch, 0, batches - 1)
        x_in = jnp.where(
            segment == 0, lax.dynamic_index_in_dim(packed, pick, 0, keepdims=False), inbox
        )
        flag_row = lax.dynamic_index_in_dim(flags, pick, 0, keepdims=False)

        def forward_active(x):
            intra = section_tables(log_rate, flag_row)
            return section(x, zero_extra, w_query, gain, intra)[0]

        def forward_resting(x):
            return zero_rows

        output = lax.cond(valid, forward_active, forward_resting, x_in)
        keep_x = jnp.where(valid, x_in, lax.dynamic_index_in_dim(saved_x, pick, 0, keepdims=False))
        saved_x = lax.dynamic_update_index_in_dim(saved_x, keep_x, pick, 0)
        inbox = shifted(output, "pipe", 1)
        return (inbox, saved_x)

    start = (zero_rows, jnp.zeros((batches, rows, width), jnp.bfloat16))
    _, saved_x = lax.fori_loop(0, ticks, forward_tick, start)

    def backward_tick(tick, carry):
        inbox, grad_total = carry
        batch = tick - (segments - 1 - segment)
        valid = (batch >= 0) & (batch < batches)
        pick = jnp.clip(batch, 0, batches - 1)
        upstream = jnp.where(
            segment == segments - 1, lax.dynamic_index_in_dim(cot, pick, 0, keepdims=False), inbox
        )
        x_in = lax.dynamic_index_in_dim(saved_x, pick, 0, keepdims=False)
        flag_row = lax.dynamic_index_in_dim(flags, pick, 0, keepdims=False)

        def backward_active(args):
            x, d_out = args
            intra = section_tables(log_rate, flag_row)

            def mixing(x_arg, e_arg):
                return section(x_arg, e_arg, w_query, gain, intra)

            _, pullback, normal_rows = jax.vjp(mixing, x, zero_extra, has_aux=True)
            d_input, d_extra = pullback(d_out)
            d_weight = jnp.einsum(
                "ltd,ltk->ldk",
                normal_rows,
                d_extra.astype(jnp.bfloat16),
                preferred_element_type=jnp.float32,
            )
            return (d_input, d_weight)

        def backward_resting(args):
            return (zero_rows, jnp.zeros((layers, width, hidden_qk), jnp.float32))

        d_x, d_weight = lax.cond(valid, backward_active, backward_resting, (x_in, upstream))
        inbox = jax.tree.map(
            lambda part, own: part.astype(own.dtype), shifted(shortened(d_x), "pipe", -1), d_x
        )
        return (inbox, grad_total + d_weight)

    grad_start = (zero_rows, jnp.zeros((layers, width, hidden_qk), jnp.float32))
    _, grad_total = lax.fori_loop(0, ticks, backward_tick, grad_start)
    full = lax.psum(grad_total, "dp")
    share = width // groups
    own_rows = lax.dynamic_slice_in_dim(full, rank * share, share, 1)
    return own_rows


MESH = pl.DeviceIdType.MESH
F32 = jnp.float32
BF16 = jnp.bfloat16


def dot(a, b, ca=1, cb=0):
    return lax.dot_general(a, b, (((ca,), (cb,)), ((), ())), preferred_element_type=F32)


def iota(shape, dim):
    return lax.broadcasted_iota(jnp.int32, shape, dim)


def as_column(row):
    n = row.shape[1]
    eye = iota((n, n), 0) == iota((n, n), 1)
    return jnp.sum(jnp.where(eye, jnp.broadcast_to(row, (n, n)), 0), axis=1, keepdims=True)


def exchange_kernel(
    groups, slot, blocks_ref, dest_ref, w_ref, gain_ref, decay_ref,
    recv_ref, w_all, gain_all, decay_all, out_s, send_sem, recv_sem, par_send, par_recv, own_sem,
):
    me = lax.axis_index("dp")
    core = lax.axis_index("pipe")
    barrier = pltpu.get_barrier_semaphore()

    def greet(k, carry):
        pl.semaphore_signal(
            barrier, inc=1, device_id=(lax.rem(me + k, groups), core), device_id_type=MESH
        )
        return carry

    lax.fori_loop(1, groups, greet, 0)
    pl.semaphore_signal(barrier, inc=1, device_id=(me, 1 - core), device_id_type=MESH)

    own_copies = []
    for i, (src, dst) in enumerate(((w_ref, w_all), (gain_ref, gain_all), (decay_ref, decay_all))):
        own = pltpu.make_async_copy(src, dst.at[core], own_sem.at[i])
        own.start()
        own_copies.append(own)

    rows = blocks_ref.shape[1]
    per_rank = rows // CH
    total = groups * slot
    own_row = dest_ref[core, pl.ds(me, 1), :]
    own_col = as_column(own_row)
    order = (per_rank, per_rank)
    earlier = (own_row == own_col) & (iota(order, 1) < iota(order, 0))
    before = jnp.sum(jnp.where(earlier, 1, 0), axis=1, keepdims=True)
    target = own_col * slot + before * CH
    wide = (per_rank, rows)
    spread = iota(wide, 1) // CH == iota(wide, 0)
    target_row = jnp.sum(jnp.where(spread, jnp.broadcast_to(target, wide), 0), axis=0, keepdims=True)
    target_row = target_row + iota((1, rows), 1) % CH
    send_map = jnp.where(iota((total, rows), 0) == target_row, 1.0, 0.0).astype(BF16)
    picked = dot(send_map, blocks_ref[core]).astype(BF16)
    out_s[...] = picked.reshape(out_s.shape)

    pl.semaphore_wait(barrier, groups)

    def pair_copy(k):
        there = lax.rem(me + k, groups)
        return pltpu.make_async_remote_copy(
            src_ref=out_s.at[there], dst_ref=recv_ref.at[me],
            send_sem=send_sem.at[k], recv_sem=recv_sem.at[k],
            device_id=(there, core), device_id_type=MESH,
        )

    def send(k, carry):
        pair_copy(k).start()
        return carry

    lax.fori_loop(1, groups, send, 0)
    part_copies = []
    for i, (src, dst) in enumerate(((w_ref, w_all), (gain_ref, gain_all), (decay_ref, decay_all))):
        part = pltpu.make_async_remote_copy(
            src_ref=src, dst_ref=dst.at[core], send_sem=par_send.at[i], recv_sem=par_recv.at[i],
            device_id=(me, 1 - core), device_id_type=MESH,
        )
        part.start()
        part_copies.append(part)
    recv_ref[me] = out_s[me]
    for own in own_copies:
        own.wait()

    def arrive(k, carry):
        pair_copy(k).wait()
        return carry

    lax.fori_loop(1, groups, arrive, 0)
    for part in part_copies:
        part.wait()


def layers_kernel(
    heads, slot, recv_ref, dest_ref, resets_ref, w_ref, gain_ref, decay_ref, cot_ref,
    z_ref, g_ref, q_s, x_s, a_s, table_s, n_s, ro_s, r_s, dy_s, dv_s,
):
    me = lax.axis_index("dp")
    core = lax.axis_index("pipe")
    layers, rows, width = z_ref.shape
    depth = w_ref.shape[1]
    dk = g_ref.shape[2] // heads
    dv = width // heads
    per_rank = rows // CH
    groups = dest_ref.shape[1]

    hits = jnp.where(dest_ref[core] == me, 1.0, 0.0)
    order = (per_rank, per_rank)
    upper = jnp.where(iota(order, 0) < iota(order, 1), 1.0, 0.0).astype(BF16)
    before = dot(hits.astype(BF16), upper)
    sender = iota((groups, per_rank), 0).astype(F32)
    source = jnp.sum(hits * (sender * slot + before * CH), axis=0, keepdims=True)
    tall = (rows, per_rank)
    spread = iota(tall, 0) // CH == iota(tall, 1)
    source_col = jnp.sum(jnp.where(spread, jnp.broadcast_to(source, tall), 0.0), axis=1, keepdims=True)
    source_col = source_col.astype(jnp.int32) + iota((rows, 1), 0) % CH
    recv_map = jnp.where(iota((rows, groups * slot), 1) == source_col, 1.0, 0.0).astype(BF16)
    x_s[0] = dot(recv_map, recv_ref[...].reshape(groups * slot, width)).astype(BF16)

    resets = resets_ref[pl.ds(core, 1), :]
    n_resets = resets.shape[1]
    start = me * rows
    count_col = jnp.sum(
        jnp.where(resets <= iota((rows, n_resets), 0) + start, 1, 0), axis=1, keepdims=True
    )
    count_row = jnp.sum(
        jnp.where(as_column(resets) <= iota((n_resets, rows), 1) + start, 1, 0), axis=0, keepdims=True
    )
    square = (rows, rows)
    steps = iota(square, 0) - iota(square, 1)
    same = (count_col == count_row) & (steps >= 0)
    diff = steps.astype(F32)

    def forward(l, carry):
        x32 = x_s[l].astype(F32)
        scale = lax.rsqrt(jnp.mean(x32 * x32, axis=1, keepdims=True) + EPS)
        r_s[l] = scale
        gain = gain_ref[l // depth, pl.ds(l % depth, 1), :]
        z = (x32 * scale * gain).astype(BF16)
        z_ref[l] = z
        q = dot(z, w_ref[l // depth, l % depth]).astype(BF16)
        q_s[l] = q
        rates = jnp.log(decay_ref[l // depth, pl.ds(l % depth, 1), :])
        for h in range(heads):
            table = jnp.where(same, jnp.exp(diff * rates[:, h : h + 1]), 0.0)
            table_s[l, h] = table
            qh = q[:, h * dk : (h + 1) * dk]
            a = (dot(qh, qh, 1, 1) * table).astype(BF16)
            a_s[l, h] = a
            cols = slice(h * dv, (h + 1) * dv)
            o = dot(a, z[:, cols])
            ro = lax.rsqrt(jnp.mean(o * o, axis=1, keepdims=True) + EPS)
            n = o * ro
            n_s[l, :, cols] = n
            ro_s[l, h] = ro
            x_s[l + 1, :, cols] = (x32[:, cols] + n).astype(BF16)
        return carry

    lax.fori_loop(0, layers, forward, 0)
    dy_s[...] = cot_ref[core]

    def backward(i, carry):
        l = layers - 1 - i
        for h in range(heads):
            cols = slice(h * dv, (h + 1) * dv)
            dn = dy_s[:, cols].astype(F32)
            n = n_s[l, :, cols]
            do = ro_s[l, h] * (dn - n * jnp.mean(dn * n, axis=1, keepdims=True))
            do = do.astype(BF16)
            da = dot(do, z_ref[l, :, cols], 1, 1)
            ds = (da * table_s[l, h]).astype(BF16)
            dv_s[:, cols] = dot(a_s[l, h], do, 0, 0)
            qh = q_s[l, :, h * dk : (h + 1) * dk]
            g_ref[l, :, h * dk : (h + 1) * dk] = (dot(ds, qh) + dot(ds, qh, 0, 0)).astype(BF16)

        @pl.when(l > 0)
        def _():
            dz = dot(g_ref[l], w_ref[l // depth, l % depth], 1, 1) + dv_s[...]
            gain = gain_ref[l // depth, pl.ds(l % depth, 1), :]
            scale = r_s[l]
            unit = x_s[l].astype(F32) * scale
            dzg = dz * gain
            dx = scale * (dzg - unit * jnp.mean(dzg * unit, axis=1, keepdims=True))
            dy_s[...] = (dy_s[...].astype(F32) + dx).astype(BF16)

        return carry

    lax.fori_loop(0, layers, backward, 0)


def reduce_kernel(
    z_ref, g_ref, out_ref, zr_s, gr_s, part_s, r1_s, h_s, r2_s, k_s, r3_s,
    core_send, core_recv, s1_send, s1_recv, s2_send, s2_recv, s3_send, s3_recv,
):
    me = lax.axis_index("dp")
    core = lax.axis_index("pipe")
    depth, share, hidden = out_ref.shape
    nz = k_s.shape[1]
    half = hidden // 2
    x = me % 2
    y = (me // 2) % 2
    z = me // 4
    x_mate = me + 1 - 2 * x
    y_mate = me + 2 * (1 - 2 * y)
    barrier = pltpu.get_barrier_semaphore()
    mates = [(x_mate, core), (y_mate, core), (me, 1 - core)]
    mates += [(((z + k) % nz) * 4 + me % 4, core) for k in range(1, nz)]
    for mate in mates:
        pl.semaphore_signal(barrier, inc=1, device_id=mate, device_id_type=MESH)
    pl.semaphore_wait(barrier, len(mates))

    def remote(src, dst, send, recv, mate):
        return pltpu.make_async_remote_copy(
            src_ref=src, dst_ref=dst, send_sem=send, recv_sem=recv,
            device_id=mate, device_id_type=MESH,
        )

    sent = []
    cores = []
    for s in range(depth):
        theirs = (1 - core) * depth + s
        pair = []
        for i, (src, dst) in enumerate(((z_ref, zr_s), (g_ref, gr_s))):
            copy = remote(
                src.at[theirs], dst.at[s], core_send.at[s, i], core_recv.at[s, i], (me, 1 - core)
            )
            copy.start()
            pair.append(copy)
        cores.append(pair)
        sent += pair

    pieces = [(s, c) for c in range(2) for s in range(depth)]
    first = []
    for p, (s, c) in enumerate(pieces):
        if c == 0:
            for copy in cores[s]:
                copy.wait_recv()
        cols = slice(c * half, (c + 1) * half)
        mine = core * depth + s
        part = dot(z_ref[mine], g_ref[mine, :, cols], 0, 0) + dot(zr_s[s], gr_s[s, :, cols], 0, 0)
        part_s[p] = part.astype(BF16).reshape(nz, 2, 2, share, half)
        if s % 2 == 0:
            copy = remote(part_s.at[p, :, :, 1 - x], r1_s.at[p], s1_send.at[p], s1_recv.at[p], (x_mate, core))
        else:
            copy = remote(part_s.at[p, :, 1 - y], r1_s.at[p], s1_send.at[p], s1_recv.at[p], (y_mate, core))
        copy.start()
        first.append(copy)
    second = []
    for p, (s, c) in enumerate(pieces):
        first[p].wait_recv()
        if s % 2 == 0:
            there, mate = 1 - y, (y_mate, core)
            own = part_s[p, :, there, x]
        else:
            there, mate = 1 - x, (x_mate, core)
            own = part_s[p, :, y, there]
        h_s[p] = (own.astype(F32) + r1_s[p, :, there].astype(F32)).astype(BF16)
        copy = remote(h_s.at[p], r2_s.at[p], s2_send.at[p], s2_recv.at[p], mate)
        copy.start()
        second.append(copy)
    third = []
    for p, (s, c) in enumerate(pieces):
        second[p].wait_recv()
        here = y if s % 2 == 0 else x
        total = part_s[p, :, y, x].astype(F32) + r1_s[p, :, here].astype(F32)
        k_s[p] = (total + r2_s[p].astype(F32)).astype(BF16)
        row = []
        for k in range(1, nz):
            there = (z + k) % nz
            copy = remote(
                k_s.at[p, there], r3_s.at[p, k - 1], s3_send.at[p, k - 1], s3_recv.at[p, k - 1],
                (there * 4 + me % 4, core),
            )
            copy.start()
            row.append(copy)
        third.append(row)
    for p, (s, c) in enumerate(pieces):
        total = k_s[p, z].astype(F32)
        for k in range(1, nz):
            third[p][k - 1].wait_recv()
            total = total + r3_s[p, k - 1].astype(F32)
        out_ref[s, :, c * half : (c + 1) * half] = total
    for copy in sent + first + second + [copy for row in third for copy in row]:
        copy.wait_send()


def split_batches(blocks, dest, resets, w_query, gain, decay, cot):
    groups = lax.axis_size("dp")
    segments = lax.axis_size("pipe")
    _, rows, width = blocks.shape
    depth, _, hidden = w_query.shape
    heads = decay.shape[1]
    layers = depth * segments
    room = (rows // CH + groups - 1) // groups
    slot = (room * CH + 15) // 16 * 16
    vmem = pl.BlockSpec(memory_space=pltpu.VMEM)
    hbm = pl.BlockSpec(memory_space=pl.ANY)
    dma = pltpu.SemaphoreType.DMA
    limit = 50 * 2**20
    received, w_all, gain_all, decay_all = pl.pallas_call(
        functools.partial(exchange_kernel, groups, slot),
        out_shape=(
            jax.ShapeDtypeStruct((groups, slot, width), BF16),
            jax.ShapeDtypeStruct((segments,) + w_query.shape, BF16),
            jax.ShapeDtypeStruct((segments,) + gain.shape, F32),
            jax.ShapeDtypeStruct((segments,) + decay.shape, F32),
        ),
        in_specs=[vmem, vmem, hbm, vmem, vmem],
        out_specs=(vmem, hbm, vmem, vmem),
        scratch_shapes=[
            pltpu.VMEM((groups, slot, width), BF16),
            dma((groups,)), dma((groups,)), dma((3,)), dma((3,)), dma((3,)),
        ],
        compiler_params=pltpu.CompilerParams(
            collective_id=0, has_side_effects=True, vmem_limit_bytes=limit
        ),
        name="exchange",
    )(blocks, dest, w_query, gain, decay)
    z_all, g_all = pl.pallas_call(
        functools.partial(layers_kernel, heads, slot),
        out_shape=(
            jax.ShapeDtypeStruct((layers, rows, width), BF16),
            jax.ShapeDtypeStruct((layers, rows, hidden), BF16),
        ),
        in_specs=[vmem] * 7,
        out_specs=(vmem, vmem),
        scratch_shapes=[
            pltpu.VMEM((layers, rows, hidden), BF16),
            pltpu.VMEM((layers + 1, rows, width), BF16),
            pltpu.VMEM((layers, heads, rows, rows), BF16),
            pltpu.VMEM((layers, heads, rows, rows), F32),
            pltpu.VMEM((layers, rows, width), F32),
            pltpu.VMEM((layers, heads, rows, 1), F32),
            pltpu.VMEM((layers, rows, 1), F32),
            pltpu.VMEM((rows, width), BF16),
            pltpu.VMEM((rows, width), F32),
        ],
        compiler_params=pltpu.CompilerParams(vmem_limit_bytes=limit),
        name="layers",
    )(received, dest, resets, w_all, gain_all, decay_all, cot)
    share = width // groups
    nz = groups // 4
    pieces = 2 * depth
    half = hidden // 2
    return pl.pallas_call(
        reduce_kernel,
        out_shape=jax.ShapeDtypeStruct((depth, share, hidden), F32),
        in_specs=[vmem, vmem],
        out_specs=vmem,
        scratch_shapes=[
            pltpu.VMEM((depth, rows, width), BF16),
            pltpu.VMEM((depth, rows, hidden), BF16),
            pltpu.VMEM((pieces, nz, 2, 2, share, half), BF16),
            pltpu.VMEM((pieces, nz, 2, share, half), BF16),
            pltpu.VMEM((pieces, nz, share, half), BF16),
            pltpu.VMEM((pieces, nz, share, half), BF16),
            pltpu.VMEM((pieces, nz, share, half), BF16),
            pltpu.VMEM((pieces, nz - 1, share, half), BF16),
            dma((depth, 2)), dma((depth, 2)),
            dma((pieces,)), dma((pieces,)), dma((pieces,)), dma((pieces,)),
            dma((pieces, nz - 1)), dma((pieces, nz - 1)),
        ],
        compiler_params=pltpu.CompilerParams(
            collective_id=1, has_side_effects=True, vmem_limit_bytes=limit
        ),
        name="reduce",
    )(z_all, g_all)


def local(blocks, dest, resets, w_query, gain, decay, cot):
    groups = lax.axis_size("dp")
    segments = lax.axis_size("pipe")
    if segments == 2 and blocks.shape[0] == segments and groups == 16:
        return split_batches(blocks, dest, resets, w_query, gain, decay, cot)
    return pipelined(blocks, dest, resets, w_query, gain, decay, cot)


def solution(mesh):
    placed = (
        P(None, "dp", None),
        P(),
        P(),
        P("pipe", None, None),
        P("pipe", None),
        P("pipe", None),
        P(None, "dp", None),
    )
    return jax.shard_map(
        local, mesh=mesh, in_specs=placed, out_specs=P("pipe", "dp", None), check_vma=False
    )
```

```python
import functools

import jax
import jax.numpy as jnp
from jax import lax
from jax.experimental import pallas as pl
from jax.experimental.pallas import tpu as pltpu
from jax.sharding import PartitionSpec as P

CH = 4


EPS = 1e-05


def shifted(x, axis, by):
    devices = lax.axis_size(axis)
    pairs = [(i, i + by) for i in range(devices) if 0 <= i + by < devices]
    return lax.ppermute(x, axis, pairs)


def shortened(x):

    def short(part):
        return part.astype(jnp.bfloat16) if part.dtype == jnp.float32 else part

    return jax.tree.map(short, x)


def normed_project(x, weight, gain, extra):
    x32 = x.astype(jnp.float32)
    scale = lax.rsqrt(jnp.mean(x32 * x32, axis=-1, keepdims=True) + EPS)
    z = (x32 * scale * gain).astype(jnp.bfloat16)
    q = (jnp.dot(z, weight, preferred_element_type=jnp.float32) + extra).astype(jnp.bfloat16)
    return (z, q)


def tables(log_rate, flags):
    count = jnp.cumsum(flags)
    index = jnp.arange(flags.shape[0]).astype(jnp.float32)
    diff = index[:, None] - index[None, :]
    same = (count[:, None] == count[None, :]) & (diff >= 0)
    return jnp.where(same[None], jnp.exp(diff[None] * log_rate[:, None, None]), 0.0)


def section_tables(log_rate, flags):
    length = flags.shape[0]
    intra = tables(log_rate.reshape(-1), flags)
    return intra.reshape(log_rate.shape[0], log_rate.shape[1], length, length)


def finish(x, heads_out):
    normal = heads_out * lax.rsqrt(jnp.mean(heads_out * heads_out, axis=-1, keepdims=True) + EPS)
    return (x.astype(jnp.float32) + normal.reshape(x.shape)).astype(jnp.bfloat16)


def local_layer(x, extra, weight, gain_row, intra):
    z, q = normed_project(x, weight, gain_row, extra)
    heads = intra.shape[0]
    length = x.shape[0]
    query_rows = q.astype(jnp.float32).reshape(length, heads, -1)
    value_rows = z.reshape(length, heads, -1)
    scores = jnp.einsum("thk,shk->hts", query_rows, query_rows) * intra
    mixing_weights = scores.astype(jnp.bfloat16)
    outputs = jnp.einsum(
        "hts,shv->thv", mixing_weights, value_rows, preferred_element_type=jnp.float32
    )
    return (finish(x, outputs), z)


def section(x, extras, weight, gain, intra):
    normals = []
    for depth in range(weight.shape[0]):
        x, z = local_layer(x, extras[depth], weight[depth], gain[depth], intra[depth])
        normals.append(z)
    return (x, jnp.stack(normals))


def pipelined(blocks, dest, resets, w_query, gain, decay, cot):
    groups = lax.axis_size("dp")
    segments = lax.axis_size("pipe")
    rank = lax.axis_index("dp")
    segment = lax.axis_index("pipe")
    batches, rows, width = blocks.shape
    per_rank = rows // CH
    room = (per_rank + groups - 1) // groups
    mine = blocks.reshape(batches, per_rank, CH * width)
    own = lax.dynamic_index_in_dim(dest, rank, 1, keepdims=False)
    order = jnp.arange(per_rank)
    before_mask = order[None, :] < order[:, None]
    matching = own[:, :, None] == own[:, None, :]
    before = jnp.sum((matching & before_mask[None]).astype(jnp.int32), axis=2)
    target = own * room + before
    slot_ids = jnp.arange(groups * room, dtype=jnp.int32)
    send_map = (target[:, None, :] == slot_ids[None, :, None]).astype(jnp.bfloat16)
    outgoing = jnp.einsum(
        "mtj,mjc->mtc", send_map, mine, preferred_element_type=jnp.float32
    ).astype(jnp.bfloat16)
    incoming = lax.all_to_all(outgoing, "dp", split_axis=1, concat_axis=1, tiled=True)
    hits = (dest == rank).astype(jnp.int32)
    rank_in = jnp.cumsum(hits, axis=2) - 1
    senders = jnp.arange(groups, dtype=jnp.int32)[None, :, None]
    source = jnp.sum(hits * (senders * room + rank_in), axis=1)
    recv_map = (source[:, :, None] == slot_ids[None, None, :]).astype(jnp.bfloat16)
    packed = (
        jnp.einsum("mjt,mtc->mjc", recv_map, incoming, preferred_element_type=jnp.float32)
        .astype(jnp.bfloat16)
        .reshape(batches, rows, width)
    )
    positions = rank * rows + jnp.arange(rows, dtype=jnp.int32)
    flags = jnp.any(positions[None, :, None] == resets[:, None, :], axis=-1).astype(jnp.float32)
    layers = w_query.shape[0]
    hidden_qk = w_query.shape[2]
    log_rate = jnp.log(decay)
    zero_extra = jnp.zeros((layers, rows, hidden_qk), jnp.float32)
    zero_rows = jnp.zeros((rows, width), jnp.bfloat16)
    ticks = batches + segments - 1

    def forward_tick(tick, carry):
        inbox, saved_x = carry
        batch = tick - segment
        valid = (batch >= 0) & (batch < batches)
        pick = jnp.clip(batch, 0, batches - 1)
        x_in = jnp.where(
            segment == 0, lax.dynamic_index_in_dim(packed, pick, 0, keepdims=False), inbox
        )
        flag_row = lax.dynamic_index_in_dim(flags, pick, 0, keepdims=False)

        def forward_active(x):
            intra = section_tables(log_rate, flag_row)
            return section(x, zero_extra, w_query, gain, intra)[0]

        def forward_resting(x):
            return zero_rows

        output = lax.cond(valid, forward_active, forward_resting, x_in)
        keep_x = jnp.where(valid, x_in, lax.dynamic_index_in_dim(saved_x, pick, 0, keepdims=False))
        saved_x = lax.dynamic_update_index_in_dim(saved_x, keep_x, pick, 0)
        inbox = shifted(output, "pipe", 1)
        return (inbox, saved_x)

    start = (zero_rows, jnp.zeros((batches, rows, width), jnp.bfloat16))
    _, saved_x = lax.fori_loop(0, ticks, forward_tick, start)

    def backward_tick(tick, carry):
        inbox, grad_total = carry
        batch = tick - (segments - 1 - segment)
        valid = (batch >= 0) & (batch < batches)
        pick = jnp.clip(batch, 0, batches - 1)
        upstream = jnp.where(
            segment == segments - 1, lax.dynamic_index_in_dim(cot, pick, 0, keepdims=False), inbox
        )
        x_in = lax.dynamic_index_in_dim(saved_x, pick, 0, keepdims=False)
        flag_row = lax.dynamic_index_in_dim(flags, pick, 0, keepdims=False)

        def backward_active(args):
            x, d_out = args
            intra = section_tables(log_rate, flag_row)

            def mixing(x_arg, e_arg):
                return section(x_arg, e_arg, w_query, gain, intra)

            _, pullback, normal_rows = jax.vjp(mixing, x, zero_extra, has_aux=True)
            d_input, d_extra = pullback(d_out)
            d_weight = jnp.einsum(
                "ltd,ltk->ldk",
                normal_rows,
                d_extra.astype(jnp.bfloat16),
                preferred_element_type=jnp.float32,
            )
            return (d_input, d_weight)

        def backward_resting(args):
            return (zero_rows, jnp.zeros((layers, width, hidden_qk), jnp.float32))

        d_x, d_weight = lax.cond(valid, backward_active, backward_resting, (x_in, upstream))
        inbox = jax.tree.map(
            lambda part, own: part.astype(own.dtype), shifted(shortened(d_x), "pipe", -1), d_x
        )
        return (inbox, grad_total + d_weight)

    grad_start = (zero_rows, jnp.zeros((layers, width, hidden_qk), jnp.float32))
    _, grad_total = lax.fori_loop(0, ticks, backward_tick, grad_start)
    full = lax.psum(grad_total, "dp")
    share = width // groups
    own_rows = lax.dynamic_slice_in_dim(full, rank * share, share, 1)
    return own_rows


MESH = pl.DeviceIdType.MESH
F32 = jnp.float32
BF16 = jnp.bfloat16


def dot(a, b, ca=1, cb=0):
    return lax.dot_general(a, b, (((ca,), (cb,)), ((), ())), preferred_element_type=F32)


def iota(shape, dim):
    return lax.broadcasted_iota(jnp.int32, shape, dim)


def as_column(row):
    n = row.shape[1]
    eye = iota((n, n), 0) == iota((n, n), 1)
    return jnp.sum(jnp.where(eye, jnp.broadcast_to(row, (n, n)), 0), axis=1, keepdims=True)


def exchange_kernel(
    groups, slot, blocks_ref, dest_ref, w_ref, gain_ref, decay_ref,
    recv_ref, w_all, gain_all, decay_all,
    in_s, dest_s, out_s, in_sem, send_sem, recv_sem, par_send, par_recv, own_sem,
):
    me = lax.axis_index("dp")
    core = lax.axis_index("pipe")
    barrier = pltpu.get_barrier_semaphore()
    loads = [
        pltpu.make_async_copy(dest_ref.at[core], dest_s, in_sem.at[0]),
        pltpu.make_async_copy(blocks_ref.at[core], in_s, in_sem.at[1]),
    ]
    for load in loads:
        load.start()

    def greet(k, carry):
        pl.semaphore_signal(
            barrier, inc=1, device_id=(lax.rem(me + k, groups), core), device_id_type=MESH
        )
        return carry

    lax.fori_loop(1, groups, greet, 0)
    pl.semaphore_signal(barrier, inc=1, device_id=(me, 1 - core), device_id_type=MESH)

    own_copies = []
    for i, (src, dst) in enumerate(((w_ref, w_all), (gain_ref, gain_all), (decay_ref, decay_all))):
        own = pltpu.make_async_copy(src, dst.at[core], own_sem.at[i])
        own.start()
        own_copies.append(own)

    rows = blocks_ref.shape[1]
    per_rank = rows // CH
    total = groups * slot
    loads[0].wait()
    own_row = dest_s[pl.ds(me, 1), :]
    own_col = as_column(own_row)
    order = (per_rank, per_rank)
    earlier = (own_row == own_col) & (iota(order, 1) < iota(order, 0))
    before = jnp.sum(jnp.where(earlier, 1, 0), axis=1, keepdims=True)
    target = own_col * slot + before * CH
    wide = (per_rank, rows)
    spread = iota(wide, 1) // CH == iota(wide, 0)
    target_row = jnp.sum(jnp.where(spread, jnp.broadcast_to(target, wide), 0), axis=0, keepdims=True)
    target_row = target_row + iota((1, rows), 1) % CH
    send_map = jnp.where(iota((total, rows), 0) == target_row, 1.0, 0.0).astype(BF16)
    loads[1].wait()
    picked = dot(send_map, in_s[...]).astype(BF16)
    out_s[...] = picked.reshape(out_s.shape)

    pl.semaphore_wait(barrier, groups)

    def pair_copy(k):
        there = lax.rem(me + k, groups)
        return pltpu.make_async_remote_copy(
            src_ref=out_s.at[there], dst_ref=recv_ref.at[me],
            send_sem=send_sem.at[k], recv_sem=recv_sem.at[k],
            device_id=(there, core), device_id_type=MESH,
        )

    def send(k, carry):
        pair_copy(k).start()
        return carry

    lax.fori_loop(1, groups, send, 0)
    part_copies = []
    for i, (src, dst) in enumerate(((w_ref, w_all), (gain_ref, gain_all), (decay_ref, decay_all))):
        part = pltpu.make_async_remote_copy(
            src_ref=src, dst_ref=dst.at[core], send_sem=par_send.at[i], recv_sem=par_recv.at[i],
            device_id=(me, 1 - core), device_id_type=MESH,
        )
        part.start()
        part_copies.append(part)
    recv_ref[me] = out_s[me]
    for own in own_copies:
        own.wait()

    def arrive(k, carry):
        pair_copy(k).wait()
        return carry

    lax.fori_loop(1, groups, arrive, 0)
    for part in part_copies:
        part.wait()


def layers_kernel(
    heads, slot, recv_ref, dest_ref, resets_ref, w_ref, gain_ref, decay_ref, cot_ref, out_ref,
    dest_s, resets_s, z_s, g_s, q_s, x_s, a_s, table_s, n_s, ro_s, r_s, dy_s, dv_s,
    zr_s, gr_s, part_s, r1_s, h_s, r2_s, k_s, r3_s, fin_s, finr_s,
    in_sem, z_send, z_recv, g_send, g_recv, s1_send, s1_recv, s2_send, s2_recv,
    s3_send, s3_recv, f_send, f_recv,
):
    me = lax.axis_index("dp")
    core = lax.axis_index("pipe")
    layers, rows, width = z_s.shape
    depth, share, hidden = out_ref.shape
    half = hidden // 2
    nz = k_s.shape[1]
    dk = hidden // heads
    dv = width // heads
    per_rank = rows // CH
    groups = dest_ref.shape[1]
    x = me % 2
    y = (me // 2) % 2
    z_at = me // 4
    x_mate = me + 1 - 2 * x
    y_mate = me + 2 * (1 - 2 * y)
    peer = (me, 1 - core)
    loads = [
        pltpu.make_async_copy(dest_ref.at[core], dest_s, in_sem.at[0]),
        pltpu.make_async_copy(resets_ref, resets_s, in_sem.at[1]),
        pltpu.make_async_copy(cot_ref.at[core], dy_s, in_sem.at[2]),
    ]
    for load in loads:
        load.start()
    barrier = pltpu.get_barrier_semaphore()
    mates = [(x_mate, core), (y_mate, core), peer]
    mates += [(((z_at + k) % nz) * 4 + me % 4, core) for k in range(1, nz)]
    for mate in mates:
        pl.semaphore_signal(barrier, inc=1, device_id=mate, device_id_type=MESH)

    def remote(src, dst, send, recv, mate):
        return pltpu.make_async_remote_copy(
            src_ref=src, dst_ref=dst, send_sem=send, recv_sem=recv,
            device_id=mate, device_id_type=MESH,
        )

    def z_copy(l):
        return remote(z_s.at[l], zr_s.at[l], z_send.at[l], z_recv.at[l], peer)

    loads[0].wait()
    hits = jnp.where(dest_s[...] == me, 1.0, 0.0)
    order = (per_rank, per_rank)
    upper = jnp.where(iota(order, 0) < iota(order, 1), 1.0, 0.0).astype(BF16)
    before = dot(hits.astype(BF16), upper)
    sender = iota((groups, per_rank), 0).astype(F32)
    source = jnp.sum(hits * (sender * slot + before * CH), axis=0, keepdims=True)
    tall = (rows, per_rank)
    spread = iota(tall, 0) // CH == iota(tall, 1)
    source_col = jnp.sum(jnp.where(spread, jnp.broadcast_to(source, tall), 0.0), axis=1, keepdims=True)
    source_col = source_col.astype(jnp.int32) + iota((rows, 1), 0) % CH
    recv_map = jnp.where(iota((rows, groups * slot), 1) == source_col, 1.0, 0.0).astype(BF16)
    x_s[0] = dot(recv_map, recv_ref[...].reshape(groups * slot, width)).astype(BF16)

    loads[1].wait()
    resets = resets_s[pl.ds(core, 1), :]
    n_resets = resets.shape[1]
    start = me * rows
    count_col = jnp.sum(
        jnp.where(resets <= iota((rows, n_resets), 0) + start, 1, 0), axis=1, keepdims=True
    )
    count_row = jnp.sum(
        jnp.where(as_column(resets) <= iota((n_resets, rows), 1) + start, 1, 0), axis=0, keepdims=True
    )
    square = (rows, rows)
    steps = iota(square, 0) - iota(square, 1)
    same = (count_col == count_row) & (steps >= 0)
    diff = steps.astype(F32)

    pl.semaphore_wait(barrier, len(mates))

    def forward(l, carry):
        x32 = x_s[l].astype(F32)
        scale = lax.rsqrt(jnp.mean(x32 * x32, axis=1, keepdims=True) + EPS)
        r_s[l] = scale
        gain = gain_ref[l // depth, pl.ds(l % depth, 1), :]
        z = (x32 * scale * gain).astype(BF16)
        z_s[l] = z
        z_copy(l).start()
        q = dot(z, w_ref[l // depth, l % depth]).astype(BF16)
        q_s[l] = q
        rates = jnp.log(decay_ref[l // depth, pl.ds(l % depth, 1), :])
        for h in range(heads):
            table = jnp.where(same, jnp.exp(diff * rates[:, h : h + 1]), 0.0)
            table_s[l, h] = table
            qh = q[:, h * dk : (h + 1) * dk]
            a = (dot(qh, qh, 1, 1) * table).astype(BF16)
            a_s[l, h] = a
            cols = slice(h * dv, (h + 1) * dv)
            o = dot(a, z[:, cols])
            ro = lax.rsqrt(jnp.mean(o * o, axis=1, keepdims=True) + EPS)
            n = o * ro
            n_s[l, :, cols] = n
            ro_s[l, h] = ro
            x_s[l + 1, :, cols] = (x32[:, cols] + n).astype(BF16)
        return carry

    lax.fori_loop(0, layers, forward, 0)
    loads[2].wait()
    copies = {}

    def begin(name, copy):
        copy.start()
        copies[name] = copy

    def places(l):
        by_x = (core + l) % 2
        by_y = 1 - by_x
        first = (by_x * x_mate + by_y * y_mate, core)
        second = (by_x * y_mate + by_y * x_mate, core)
        return by_x, by_y, by_x * x + by_y * y, by_x * y + by_y * x, first, second

    def weight_part(l):
        by_x, by_y, f, s, first, second = places(l)
        copies["g", l].wait_recv()
        z_copy(l).wait_recv()
        part = dot(z_s[l], g_s[l, core], 0, 0) + dot(zr_s[l], gr_s[l], 0, 0)
        for d in range(groups):
            zd, yd, xd = d // 4, (d // 2) % 2, d % 2
            rows_d = part[d * share : (d + 1) * share].astype(BF16)
            part_s[l, by_x * xd + by_y * yd, by_x * yd + by_y * xd, zd] = rows_d
        begin(("s1", l), remote(part_s.at[l, 1 - f], r1_s.at[l], s1_send.at[l], s1_recv.at[l], first))

    def stage_two(l):
        _, _, f, s, first, second = places(l)
        copies["s1", l].wait_recv()
        total = part_s[l, f, 1 - s].astype(F32) + r1_s[l, 1 - s].astype(F32)
        h_s[l] = total.astype(BF16)
        begin(("s2", l), remote(h_s.at[l], r2_s.at[l], s2_send.at[l], s2_recv.at[l], second))

    def stage_three(l):
        _, _, f, s, first, second = places(l)
        copies["s2", l].wait_recv()
        total = part_s[l, f, s].astype(F32) + r1_s[l, s].astype(F32) + r2_s[l].astype(F32)
        k_s[l] = total.astype(BF16)
        for k in range(1, nz):
            there = (z_at + k) % nz
            begin(("s3", l, k), remote(
                k_s.at[l, there], r3_s.at[l, k - 1], s3_send.at[l, k - 1], s3_recv.at[l, k - 1],
                (there * 4 + me % 4, core),
            ))

    def finish_sum(l):
        total = k_s[l, z_at].astype(F32)
        for k in range(1, nz):
            copies["s3", l, k].wait_recv()
            total = total + r3_s[l, k - 1].astype(F32)
        fin_s[l] = total

    def backward(l):
        for h in range(heads):
            cols = slice(h * dv, (h + 1) * dv)
            dn = dy_s[:, cols].astype(F32)
            n = n_s[l, :, cols]
            do = ro_s[l, h] * (dn - n * jnp.mean(dn * n, axis=1, keepdims=True))
            do = do.astype(BF16)
            da = dot(do, z_s[l, :, cols], 1, 1)
            ds = (da * table_s[l, h]).astype(BF16)
            if l > 0:
                dv_s[:, cols] = dot(a_s[l, h], do, 0, 0)
            qh = q_s[l, :, h * dk : (h + 1) * dk]
            at = h * dk % half
            g_s[l, h * dk // half, :, at : at + dk] = (dot(ds, qh) + dot(ds, qh, 0, 0)).astype(BF16)
        begin(("g", l), remote(g_s.at[l, 1 - core], gr_s.at[l], g_send.at[l], g_recv.at[l], peer))
        if l > 0:
            w = w_ref[l // depth, l % depth]
            dz = dot(g_s[l, 0], w[:, :half], 1, 1) + dot(g_s[l, 1], w[:, half:], 1, 1) + dv_s[...]
            gain = gain_ref[l // depth, pl.ds(l % depth, 1), :]
            scale = r_s[l]
            unit = x_s[l].astype(F32) * scale
            dzg = dz * gain
            dx = scale * (dzg - unit * jnp.mean(dzg * unit, axis=1, keepdims=True))
            dy_s[...] = (dy_s[...].astype(F32) + dx).astype(BF16)

    for step in range(layers + 3):
        l = layers - 1 - step
        if l >= 0:
            backward(l)
            weight_part(l)
        if 0 <= l + 1 < layers:
            stage_two(l + 1)
        if 0 <= l + 2 < layers:
            stage_three(l + 2)
        if 0 <= l + 3 < layers:
            finish_sum(l + 3)

    for s in range(depth):
        theirs = (1 - core) * depth + s
        begin(("f", s), remote(fin_s.at[theirs], finr_s.at[s], f_send.at[s], f_recv.at[s], peer))
    mine = pl.ds(pl.multiple_of(core * half, half), half)
    other = pl.ds(pl.multiple_of((1 - core) * half, half), half)
    for s in range(depth):
        out_ref[s, :, mine] = fin_s[core * depth + s]
    for s in range(depth):
        copies["f", s].wait_recv()
        out_ref[s, :, other] = finr_s[s]
    for copy in copies.values():
        copy.wait_send()
    for l in range(layers):
        z_copy(l).wait_send()


def split_batches(blocks, dest, resets, w_query, gain, decay, cot):
    groups = lax.axis_size("dp")
    segments = lax.axis_size("pipe")
    _, rows, width = blocks.shape
    depth, _, hidden = w_query.shape
    heads = decay.shape[1]
    layers = depth * segments
    room = (rows // CH + groups - 1) // groups
    slot = (room * CH + 15) // 16 * 16
    vmem = pl.BlockSpec(memory_space=pltpu.VMEM)
    hbm = pl.BlockSpec(memory_space=pltpu.HBM)
    dma = pltpu.SemaphoreType.DMA
    limit = 63 * 2**20
    received, w_all, gain_all, decay_all = pl.pallas_call(
        functools.partial(exchange_kernel, groups, slot),
        out_shape=(
            jax.ShapeDtypeStruct((groups, slot, width), BF16),
            jax.ShapeDtypeStruct((segments,) + w_query.shape, BF16),
            jax.ShapeDtypeStruct((segments,) + gain.shape, F32),
            jax.ShapeDtypeStruct((segments,) + decay.shape, F32),
        ),
        in_specs=[hbm] * 5,
        out_specs=(vmem, vmem, vmem, vmem),
        scratch_shapes=[
            pltpu.VMEM((rows, width), BF16),
            pltpu.VMEM(dest.shape[1:], jnp.int32),
            pltpu.VMEM((groups, slot, width), BF16),
            dma((2,)), dma((groups,)), dma((groups,)), dma((3,)), dma((3,)), dma((3,)),
        ],
        compiler_params=pltpu.CompilerParams(
            collective_id=0, has_side_effects=True, vmem_limit_bytes=limit
        ),
        name="exchange",
    )(blocks, dest, w_query, gain, decay)
    share = width // groups
    nz = groups // 4
    half = hidden // 2
    return pl.pallas_call(
        functools.partial(layers_kernel, heads, slot),
        out_shape=jax.ShapeDtypeStruct((depth, share, hidden), F32),
        in_specs=[vmem, hbm, hbm, vmem, vmem, vmem, hbm],
        out_specs=vmem,
        scratch_shapes=[
            pltpu.VMEM(dest.shape[1:], jnp.int32),
            pltpu.VMEM(resets.shape, jnp.int32),
            pltpu.VMEM((layers, rows, width), BF16),
            pltpu.VMEM((layers, 2, rows, half), BF16),
            pltpu.VMEM((layers, rows, hidden), BF16),
            pltpu.VMEM((layers + 1, rows, width), BF16),
            pltpu.VMEM((layers, heads, rows, rows), BF16),
            pltpu.VMEM((layers, heads, rows, rows), F32),
            pltpu.VMEM((layers, rows, width), F32),
            pltpu.VMEM((layers, heads, rows, 1), F32),
            pltpu.VMEM((layers, rows, 1), F32),
            pltpu.VMEM((rows, width), BF16),
            pltpu.VMEM((rows, width), F32),
            pltpu.VMEM((layers, rows, width), BF16),
            pltpu.VMEM((layers, rows, half), BF16),
            pltpu.VMEM((layers, 2, 2, nz, share, half), BF16),
            pltpu.VMEM((layers, 2, nz, share, half), BF16),
            pltpu.VMEM((layers, nz, share, half), BF16),
            pltpu.VMEM((layers, nz, share, half), BF16),
            pltpu.VMEM((layers, nz, share, half), BF16),
            pltpu.VMEM((layers, nz - 1, share, half), BF16),
            pltpu.VMEM((layers, share, half), F32),
            pltpu.VMEM((depth, share, half), F32),
            dma((3,)), dma((layers,)), dma((layers,)), dma((layers,)), dma((layers,)),
            dma((layers,)), dma((layers,)), dma((layers,)), dma((layers,)),
            dma((layers, nz - 1)), dma((layers, nz - 1)), dma((depth,)), dma((depth,)),
        ],
        compiler_params=pltpu.CompilerParams(
            collective_id=1, has_side_effects=True, vmem_limit_bytes=limit
        ),
        name="layers",
    )(received, dest, resets, w_all, gain_all, decay_all, cot)


def local(blocks, dest, resets, w_query, gain, decay, cot):
    groups = lax.axis_size("dp")
    segments = lax.axis_size("pipe")
    if segments == 2 and blocks.shape[0] == segments and groups == 16:
        return split_batches(blocks, dest, resets, w_query, gain, decay, cot)
    return pipelined(blocks, dest, resets, w_query, gain, decay, cot)


def solution(mesh):
    placed = (
        P(None, "dp", None),
        P(),
        P(),
        P("pipe", None, None),
        P("pipe", None),
        P("pipe", None),
        P(None, "dp", None),
    )
    return jax.shard_map(
        local, mesh=mesh, in_specs=placed, out_specs=P("pipe", "dp", None), check_vma=False
    )
```

```python
import functools

import jax
import jax.numpy as jnp
from jax import lax
from jax.experimental import pallas as pl
from jax.experimental.pallas import tpu as pltpu
from jax.sharding import PartitionSpec as P

CH = 4


EPS = 1e-05


def shifted(x, axis, by):
    devices = lax.axis_size(axis)
    pairs = [(i, i + by) for i in range(devices) if 0 <= i + by < devices]
    return lax.ppermute(x, axis, pairs)


def shortened(x):

    def short(part):
        return part.astype(jnp.bfloat16) if part.dtype == jnp.float32 else part

    return jax.tree.map(short, x)


def normed_project(x, weight, gain, extra):
    x32 = x.astype(jnp.float32)
    scale = lax.rsqrt(jnp.mean(x32 * x32, axis=-1, keepdims=True) + EPS)
    z = (x32 * scale * gain).astype(jnp.bfloat16)
    q = (jnp.dot(z, weight, preferred_element_type=jnp.float32) + extra).astype(jnp.bfloat16)
    return (z, q)


def tables(log_rate, flags):
    count = jnp.cumsum(flags)
    index = jnp.arange(flags.shape[0]).astype(jnp.float32)
    diff = index[:, None] - index[None, :]
    same = (count[:, None] == count[None, :]) & (diff >= 0)
    return jnp.where(same[None], jnp.exp(diff[None] * log_rate[:, None, None]), 0.0)


def section_tables(log_rate, flags):
    length = flags.shape[0]
    intra = tables(log_rate.reshape(-1), flags)
    return intra.reshape(log_rate.shape[0], log_rate.shape[1], length, length)


def finish(x, heads_out):
    normal = heads_out * lax.rsqrt(jnp.mean(heads_out * heads_out, axis=-1, keepdims=True) + EPS)
    return (x.astype(jnp.float32) + normal.reshape(x.shape)).astype(jnp.bfloat16)


def local_layer(x, extra, weight, gain_row, intra):
    z, q = normed_project(x, weight, gain_row, extra)
    heads = intra.shape[0]
    length = x.shape[0]
    query_rows = q.astype(jnp.float32).reshape(length, heads, -1)
    value_rows = z.reshape(length, heads, -1)
    scores = jnp.einsum("thk,shk->hts", query_rows, query_rows) * intra
    mixing_weights = scores.astype(jnp.bfloat16)
    outputs = jnp.einsum(
        "hts,shv->thv", mixing_weights, value_rows, preferred_element_type=jnp.float32
    )
    return (finish(x, outputs), z)


def section(x, extras, weight, gain, intra):
    normals = []
    for depth in range(weight.shape[0]):
        x, z = local_layer(x, extras[depth], weight[depth], gain[depth], intra[depth])
        normals.append(z)
    return (x, jnp.stack(normals))


def pipelined(blocks, dest, resets, w_query, gain, decay, cot):
    groups = lax.axis_size("dp")
    segments = lax.axis_size("pipe")
    rank = lax.axis_index("dp")
    segment = lax.axis_index("pipe")
    batches, rows, width = blocks.shape
    per_rank = rows // CH
    room = (per_rank + groups - 1) // groups
    mine = blocks.reshape(batches, per_rank, CH * width)
    own = lax.dynamic_index_in_dim(dest, rank, 1, keepdims=False)
    order = jnp.arange(per_rank)
    before_mask = order[None, :] < order[:, None]
    matching = own[:, :, None] == own[:, None, :]
    before = jnp.sum((matching & before_mask[None]).astype(jnp.int32), axis=2)
    target = own * room + before
    slot_ids = jnp.arange(groups * room, dtype=jnp.int32)
    send_map = (target[:, None, :] == slot_ids[None, :, None]).astype(jnp.bfloat16)
    outgoing = jnp.einsum(
        "mtj,mjc->mtc", send_map, mine, preferred_element_type=jnp.float32
    ).astype(jnp.bfloat16)
    incoming = lax.all_to_all(outgoing, "dp", split_axis=1, concat_axis=1, tiled=True)
    hits = (dest == rank).astype(jnp.int32)
    rank_in = jnp.cumsum(hits, axis=2) - 1
    senders = jnp.arange(groups, dtype=jnp.int32)[None, :, None]
    source = jnp.sum(hits * (senders * room + rank_in), axis=1)
    recv_map = (source[:, :, None] == slot_ids[None, None, :]).astype(jnp.bfloat16)
    packed = (
        jnp.einsum("mjt,mtc->mjc", recv_map, incoming, preferred_element_type=jnp.float32)
        .astype(jnp.bfloat16)
        .reshape(batches, rows, width)
    )
    positions = rank * rows + jnp.arange(rows, dtype=jnp.int32)
    flags = jnp.any(positions[None, :, None] == resets[:, None, :], axis=-1).astype(jnp.float32)
    layers = w_query.shape[0]
    hidden_qk = w_query.shape[2]
    log_rate = jnp.log(decay)
    zero_extra = jnp.zeros((layers, rows, hidden_qk), jnp.float32)
    zero_rows = jnp.zeros((rows, width), jnp.bfloat16)
    ticks = batches + segments - 1

    def forward_tick(tick, carry):
        inbox, saved_x = carry
        batch = tick - segment
        valid = (batch >= 0) & (batch < batches)
        pick = jnp.clip(batch, 0, batches - 1)
        x_in = jnp.where(
            segment == 0, lax.dynamic_index_in_dim(packed, pick, 0, keepdims=False), inbox
        )
        flag_row = lax.dynamic_index_in_dim(flags, pick, 0, keepdims=False)

        def forward_active(x):
            intra = section_tables(log_rate, flag_row)
            return section(x, zero_extra, w_query, gain, intra)[0]

        def forward_resting(x):
            return zero_rows

        output = lax.cond(valid, forward_active, forward_resting, x_in)
        keep_x = jnp.where(valid, x_in, lax.dynamic_index_in_dim(saved_x, pick, 0, keepdims=False))
        saved_x = lax.dynamic_update_index_in_dim(saved_x, keep_x, pick, 0)
        inbox = shifted(output, "pipe", 1)
        return (inbox, saved_x)

    start = (zero_rows, jnp.zeros((batches, rows, width), jnp.bfloat16))
    _, saved_x = lax.fori_loop(0, ticks, forward_tick, start)

    def backward_tick(tick, carry):
        inbox, grad_total = carry
        batch = tick - (segments - 1 - segment)
        valid = (batch >= 0) & (batch < batches)
        pick = jnp.clip(batch, 0, batches - 1)
        upstream = jnp.where(
            segment == segments - 1, lax.dynamic_index_in_dim(cot, pick, 0, keepdims=False), inbox
        )
        x_in = lax.dynamic_index_in_dim(saved_x, pick, 0, keepdims=False)
        flag_row = lax.dynamic_index_in_dim(flags, pick, 0, keepdims=False)

        def backward_active(args):
            x, d_out = args
            intra = section_tables(log_rate, flag_row)

            def mixing(x_arg, e_arg):
                return section(x_arg, e_arg, w_query, gain, intra)

            _, pullback, normal_rows = jax.vjp(mixing, x, zero_extra, has_aux=True)
            d_input, d_extra = pullback(d_out)
            d_weight = jnp.einsum(
                "ltd,ltk->ldk",
                normal_rows,
                d_extra.astype(jnp.bfloat16),
                preferred_element_type=jnp.float32,
            )
            return (d_input, d_weight)

        def backward_resting(args):
            return (zero_rows, jnp.zeros((layers, width, hidden_qk), jnp.float32))

        d_x, d_weight = lax.cond(valid, backward_active, backward_resting, (x_in, upstream))
        inbox = jax.tree.map(
            lambda part, own: part.astype(own.dtype), shifted(shortened(d_x), "pipe", -1), d_x
        )
        return (inbox, grad_total + d_weight)

    grad_start = (zero_rows, jnp.zeros((layers, width, hidden_qk), jnp.float32))
    _, grad_total = lax.fori_loop(0, ticks, backward_tick, grad_start)
    full = lax.psum(grad_total, "dp")
    share = width // groups
    own_rows = lax.dynamic_slice_in_dim(full, rank * share, share, 1)
    return own_rows


MESH = pl.DeviceIdType.MESH
F32 = jnp.float32
BF16 = jnp.bfloat16


def dot(a, b, ca=1, cb=0):
    return lax.dot_general(a, b, (((ca,), (cb,)), ((), ())), preferred_element_type=F32)


def iota(shape, dim):
    return lax.broadcasted_iota(jnp.int32, shape, dim)


def as_column(row):
    n = row.shape[1]
    eye = iota((n, n), 0) == iota((n, n), 1)
    return jnp.sum(jnp.where(eye, jnp.broadcast_to(row, (n, n)), 0), axis=1, keepdims=True)


SPLIT = 4


def begin_exchange(
    groups, slot, blocks_ref, dest_ref, w_ref, gain_ref, decay_ref,
    recv_ref, w_all, gain_all, decay_all,
    in_s, dest_s, out_s, in_sem, send_sem, recv_sem, par_send, par_recv, own_sem,
):
    me = lax.axis_index("dp")
    core = lax.axis_index("pipe")
    barrier = pltpu.get_barrier_semaphore()
    loads = [
        pltpu.make_async_copy(dest_ref.at[core], dest_s, in_sem.at[0]),
        pltpu.make_async_copy(blocks_ref.at[core], in_s, in_sem.at[1]),
    ]
    for load in loads:
        load.start()

    def greet(k, carry):
        pl.semaphore_signal(
            barrier, inc=1, device_id=(lax.rem(me + k, groups), core), device_id_type=MESH
        )
        return carry

    lax.fori_loop(1, groups, greet, 0)
    pl.semaphore_signal(barrier, inc=1, device_id=(me, 1 - core), device_id_type=MESH)

    own_copies = []
    for i, (src, dst) in enumerate(((w_ref, w_all), (gain_ref, gain_all), (decay_ref, decay_all))):
        own = pltpu.make_async_copy(src, dst.at[core], own_sem.at[i])
        own.start()
        own_copies.append(own)

    rows = blocks_ref.shape[1]
    per_rank = rows // CH
    total = groups * slot
    loads[0].wait()
    own_row = dest_s[pl.ds(me, 1), :]
    own_col = as_column(own_row)
    order = (per_rank, per_rank)
    earlier = (own_row == own_col) & (iota(order, 1) < iota(order, 0))
    before = jnp.sum(jnp.where(earlier, 1, 0), axis=1, keepdims=True)
    target = own_col * slot + before * CH
    wide = (per_rank, rows)
    spread = iota(wide, 1) // CH == iota(wide, 0)
    target_row = jnp.sum(jnp.where(spread, jnp.broadcast_to(target, wide), 0), axis=0, keepdims=True)
    target_row = target_row + iota((1, rows), 1) % CH
    loads[1].wait()
    lanes = in_s.shape[1] // SPLIT
    picked = jnp.zeros((total, lanes), F32)
    for c in range(SPLIT):
        wanted = target_row + c * (slot // SPLIT)
        send_map = jnp.where(iota((total, rows), 0) == wanted, 1.0, 0.0).astype(BF16)
        picked = picked + dot(send_map, in_s[:, c * lanes : (c + 1) * lanes])
    out_s[...] = picked.astype(BF16).reshape(out_s.shape)

    pl.semaphore_wait(barrier, groups)

    def pair_copy(k):
        there = lax.rem(me + k, groups)
        return pltpu.make_async_remote_copy(
            src_ref=out_s.at[there], dst_ref=recv_ref.at[me],
            send_sem=send_sem.at[k], recv_sem=recv_sem.at[k],
            device_id=(there, core), device_id_type=MESH,
        )

    def send(k, carry):
        pair_copy(k).start()
        return carry

    lax.fori_loop(1, groups, send, 0)
    part_copies = []
    for i, (src, dst) in enumerate(((w_ref, w_all), (gain_ref, gain_all), (decay_ref, decay_all))):
        part = pltpu.make_async_remote_copy(
            src_ref=src, dst_ref=dst.at[core], send_sem=par_send.at[i], recv_sem=par_recv.at[i],
            device_id=(me, 1 - core), device_id_type=MESH,
        )
        part.start()
        part_copies.append(part)
    recv_ref[me] = out_s[me]

    def scalars_here():
        own_copies[2].wait()
        part_copies[2].wait()

    def rest_here():
        for copy in own_copies[:2] + part_copies[:2]:
            copy.wait()

        def arrive(k, carry):
            pair_copy(k).wait()
            return carry

        lax.fori_loop(1, groups, arrive, 0)

    return scalars_here, rest_here


def layers_kernel(
    heads, slot, blocks_ref, dest_ref, resets_ref, w_own, gain_own, decay_own, cot_ref, out_ref,
    recv_ref, w_ref, gain_ref, decay_ref, blocks_s, out_s,
    blocks_sem, send_sem, recv_sem, par_send, par_recv, own_sem,
    dest_s, resets_s, z_s, g_s, q_s, x_s, a_s, table_s, n_s, ro_s, r_s, dy_s, dv_s,
    zr_s, gr_s, part_s, r1_s, h_s, r2_s, k_s, r3_s, fin_s, finr_s,
    in_sem, z_send, z_recv, g_send, g_recv, s1_send, s1_recv, s2_send, s2_recv,
    s3_send, s3_recv, f_send, f_recv,
):
    me = lax.axis_index("dp")
    core = lax.axis_index("pipe")
    layers, rows, width = z_s.shape
    depth, share, hidden = out_ref.shape
    half = hidden // 2
    nz = k_s.shape[1]
    dk = hidden // heads
    dv = width // heads
    per_rank = rows // CH
    groups = dest_ref.shape[1]
    x = me % 2
    y = (me // 2) % 2
    z_at = me // 4
    x_mate = me + 1 - 2 * x
    y_mate = me + 2 * (1 - 2 * y)
    peer = (me, 1 - core)
    loads = [
        pltpu.make_async_copy(resets_ref, resets_s, in_sem.at[0]),
        pltpu.make_async_copy(cot_ref.at[core], dy_s, in_sem.at[1]),
    ]
    for load in loads:
        load.start()
    scalars_here, rest_here = begin_exchange(
        groups, slot, blocks_ref, dest_ref, w_own, gain_own, decay_own,
        recv_ref, w_ref, gain_ref, decay_ref, blocks_s, dest_s, out_s,
        blocks_sem, send_sem, recv_sem, par_send, par_recv, own_sem,
    )

    def remote(src, dst, send, recv, mate):
        return pltpu.make_async_remote_copy(
            src_ref=src, dst_ref=dst, send_sem=send, recv_sem=recv,
            device_id=mate, device_id_type=MESH,
        )

    def z_copy(l):
        return remote(z_s.at[l], zr_s.at[l], z_send.at[l], z_recv.at[l], peer)

    hits = jnp.where(dest_s[...] == me, 1.0, 0.0)
    order = (per_rank, per_rank)
    upper = jnp.where(iota(order, 0) < iota(order, 1), 1.0, 0.0).astype(BF16)
    before = dot(hits.astype(BF16), upper)
    sender = iota((groups, per_rank), 0).astype(F32)
    source = jnp.sum(hits * (sender * slot + before * CH), axis=0, keepdims=True)
    tall = (rows, per_rank)
    spread = iota(tall, 0) // CH == iota(tall, 1)
    source_col = jnp.sum(jnp.where(spread, jnp.broadcast_to(source, tall), 0.0), axis=1, keepdims=True)
    source_col = source_col.astype(jnp.int32) + iota((rows, 1), 0) % CH
    loads[0].wait()
    resets = resets_s[pl.ds(core, 1), :]
    n_resets = resets.shape[1]
    start = me * rows
    count_col = jnp.sum(
        jnp.where(resets <= iota((rows, n_resets), 0) + start, 1, 0), axis=1, keepdims=True
    )
    count_row = jnp.sum(
        jnp.where(as_column(resets) <= iota((n_resets, rows), 1) + start, 1, 0), axis=0, keepdims=True
    )
    square = (rows, rows)
    steps = iota(square, 0) - iota(square, 1)
    same = (count_col == count_row) & (steps >= 0)
    diff = steps.astype(F32)

    scalars_here()

    def fill(l, carry):
        rates = jnp.log(decay_ref[l // depth, pl.ds(l % depth, 1), :])
        for h in range(heads):
            table_s[l, h] = jnp.where(same, jnp.exp(diff * rates[:, h : h + 1]), 0.0)
        return carry

    lax.fori_loop(0, layers, fill, 0)
    rest_here()
    lanes = width // SPLIT
    arrived = recv_ref[...].reshape(groups * slot, lanes)
    for c in range(SPLIT):
        wanted = source_col + c * (slot // SPLIT)
        recv_map = jnp.where(iota((rows, groups * slot), 1) == wanted, 1.0, 0.0).astype(BF16)
        x_s[0, :, c * lanes : (c + 1) * lanes] = dot(recv_map, arrived).astype(BF16)

    def forward(l, carry):
        x32 = x_s[l].astype(F32)
        scale = lax.rsqrt(jnp.mean(x32 * x32, axis=1, keepdims=True) + EPS)
        r_s[l] = scale
        gain = gain_ref[l // depth, pl.ds(l % depth, 1), :]
        z = (x32 * scale * gain).astype(BF16)
        z_s[l] = z
        z_copy(l).start()
        q = dot(z, w_ref[l // depth, l % depth]).astype(BF16)
        q_s[l] = q
        for h in range(heads):
            table = table_s[l, h]
            qh = q[:, h * dk : (h + 1) * dk]
            a = (dot(qh, qh, 1, 1) * table).astype(BF16)
            a_s[l, h] = a
            cols = slice(h * dv, (h + 1) * dv)
            o = dot(a, z[:, cols])
            ro = lax.rsqrt(jnp.mean(o * o, axis=1, keepdims=True) + EPS)
            n = o * ro
            n_s[l, :, cols] = n
            ro_s[l, h] = ro
            x_s[l + 1, :, cols] = (x32[:, cols] + n).astype(BF16)
        return carry

    lax.fori_loop(0, layers, forward, 0)
    loads[1].wait()
    copies = {}

    def begin(name, copy):
        copy.start()
        copies[name] = copy

    def places(l):
        by_x = (core + l) % 2
        by_y = 1 - by_x
        first = (by_x * x_mate + by_y * y_mate, core)
        second = (by_x * y_mate + by_y * x_mate, core)
        return by_x, by_y, by_x * x + by_y * y, by_x * y + by_y * x, first, second

    def weight_part(l):
        by_x, by_y, f, s, first, second = places(l)
        part = dot(z_s[l], g_s[l, core], 0, 0)
        copies["g", l].wait_recv()
        z_copy(l).wait_recv()
        part = part + dot(zr_s[l], gr_s[l], 0, 0)
        for d in range(groups):
            zd, yd, xd = d // 4, (d // 2) % 2, d % 2
            rows_d = part[d * share : (d + 1) * share].astype(BF16)
            part_s[l, by_x * xd + by_y * yd, by_x * yd + by_y * xd, zd] = rows_d
        begin(("s1", l), remote(part_s.at[l, 1 - f], r1_s.at[l], s1_send.at[l], s1_recv.at[l], first))

    def stage_two(l):
        _, _, f, s, first, second = places(l)
        copies["s1", l].wait_recv()
        total = part_s[l, f, 1 - s].astype(F32) + r1_s[l, 1 - s].astype(F32)
        h_s[l] = total.astype(BF16)
        begin(("s2", l), remote(h_s.at[l], r2_s.at[l], s2_send.at[l], s2_recv.at[l], second))

    def stage_three(l):
        _, _, f, s, first, second = places(l)
        copies["s2", l].wait_recv()
        total = part_s[l, f, s].astype(F32) + r1_s[l, s].astype(F32) + r2_s[l].astype(F32)
        k_s[l] = total.astype(BF16)
        for k in range(1, nz):
            there = (z_at + k) % nz
            begin(("s3", l, k), remote(
                k_s.at[l, there], r3_s.at[l, k - 1], s3_send.at[l, k - 1], s3_recv.at[l, k - 1],
                (there * 4 + me % 4, core),
            ))

    def finish_sum(l):
        total = k_s[l, z_at].astype(F32)
        for k in range(1, nz):
            copies["s3", l, k].wait_recv()
            total = total + r3_s[l, k - 1].astype(F32)
        fin_s[l] = total

    def backward(l):
        for h in range(heads):
            if h == heads // 2 and l + 1 < layers:
                weight_part(l + 1)
            cols = slice(h * dv, (h + 1) * dv)
            dn = dy_s[:, cols].astype(F32)
            n = n_s[l, :, cols]
            do = ro_s[l, h] * (dn - n * jnp.mean(dn * n, axis=1, keepdims=True))
            do = do.astype(BF16)
            da = dot(do, z_s[l, :, cols], 1, 1)
            ds = (da * table_s[l, h]).astype(BF16)
            if l > 0:
                dv_s[:, cols] = dot(a_s[l, h], do, 0, 0)
            qh = q_s[l, :, h * dk : (h + 1) * dk]
            at = h * dk % half
            g_s[l, h * dk // half, :, at : at + dk] = (dot(ds, qh) + dot(ds, qh, 0, 0)).astype(BF16)
        begin(("g", l), remote(g_s.at[l, 1 - core], gr_s.at[l], g_send.at[l], g_recv.at[l], peer))
        if l > 0:
            w = w_ref[l // depth, l % depth]
            dz = dot(g_s[l, 0], w[:, :half], 1, 1) + dot(g_s[l, 1], w[:, half:], 1, 1) + dv_s[...]
            gain = gain_ref[l // depth, pl.ds(l % depth, 1), :]
            scale = r_s[l]
            unit = x_s[l].astype(F32) * scale
            dzg = dz * gain
            dx = scale * (dzg - unit * jnp.mean(dzg * unit, axis=1, keepdims=True))
            dy_s[...] = (dy_s[...].astype(F32) + dx).astype(BF16)

    for step in range(layers + 4):
        l = layers - 1 - step
        if l >= 0:
            backward(l)
        if l == -1:
            weight_part(0)
        if 0 <= l + 2 < layers:
            stage_two(l + 2)
        if 0 <= l + 3 < layers:
            stage_three(l + 3)
        if 0 <= l + 4 < layers:
            finish_sum(l + 4)

    for s in range(depth):
        theirs = (1 - core) * depth + s
        begin(("f", s), remote(fin_s.at[theirs], finr_s.at[s], f_send.at[s], f_recv.at[s], peer))
    mine = pl.ds(pl.multiple_of(core * half, half), half)
    other = pl.ds(pl.multiple_of((1 - core) * half, half), half)
    for s in range(depth):
        out_ref[s, :, mine] = fin_s[core * depth + s]
    for s in range(depth):
        copies["f", s].wait_recv()
        out_ref[s, :, other] = finr_s[s]
    for copy in copies.values():
        copy.wait_send()
    for l in range(layers):
        z_copy(l).wait_send()


def split_batches(blocks, dest, resets, w_query, gain, decay, cot):
    groups = lax.axis_size("dp")
    segments = lax.axis_size("pipe")
    _, rows, width = blocks.shape
    depth, _, hidden = w_query.shape
    heads = decay.shape[1]
    layers = depth * segments
    room = (rows // CH + groups - 1) // groups
    slot = room * CH * SPLIT
    vmem = pl.BlockSpec(memory_space=pltpu.VMEM)
    hbm = pl.BlockSpec(memory_space=pltpu.HBM)
    dma = pltpu.SemaphoreType.DMA
    limit = 63 * 2**20
    share = width // groups
    nz = groups // 4
    half = hidden // 2
    return pl.pallas_call(
        functools.partial(layers_kernel, heads, slot),
        out_shape=jax.ShapeDtypeStruct((depth, share, hidden), F32),
        in_specs=[hbm] * 7,
        out_specs=vmem,
        scratch_shapes=[
            pltpu.VMEM((groups, slot, width // SPLIT), BF16),
            pltpu.VMEM((segments,) + w_query.shape, BF16),
            pltpu.VMEM((segments,) + gain.shape, F32),
            pltpu.VMEM((segments,) + decay.shape, F32),
            pltpu.VMEM((rows, width), BF16),
            pltpu.VMEM((groups, slot, width // SPLIT), BF16),
            dma((2,)), dma((groups,)), dma((groups,)), dma((3,)), dma((3,)), dma((3,)),
            pltpu.VMEM(dest.shape[1:], jnp.int32),
            pltpu.VMEM(resets.shape, jnp.int32),
            pltpu.VMEM((layers, rows, width), BF16),
            pltpu.VMEM((layers, 2, rows, half), BF16),
            pltpu.VMEM((layers, rows, hidden), BF16),
            pltpu.VMEM((layers + 1, rows, width), BF16),
            pltpu.VMEM((layers, heads, rows, rows), BF16),
            pltpu.VMEM((layers, heads, rows, rows), F32),
            pltpu.VMEM((layers, rows, width), F32),
            pltpu.VMEM((layers, heads, rows, 1), F32),
            pltpu.VMEM((layers, rows, 1), F32),
            pltpu.VMEM((rows, width), BF16),
            pltpu.VMEM((rows, width), F32),
            pltpu.VMEM((layers, rows, width), BF16),
            pltpu.VMEM((layers, rows, half), BF16),
            pltpu.VMEM((layers, 2, 2, nz, share, half), BF16),
            pltpu.VMEM((layers, 2, nz, share, half), BF16),
            pltpu.VMEM((layers, nz, share, half), BF16),
            pltpu.VMEM((layers, nz, share, half), BF16),
            pltpu.VMEM((layers, nz, share, half), BF16),
            pltpu.VMEM((layers, nz - 1, share, half), BF16),
            pltpu.VMEM((layers, share, half), F32),
            pltpu.VMEM((depth, share, half), F32),
            dma((2,)), dma((layers,)), dma((layers,)), dma((layers,)), dma((layers,)),
            dma((layers,)), dma((layers,)), dma((layers,)), dma((layers,)),
            dma((layers, nz - 1)), dma((layers, nz - 1)), dma((depth,)), dma((depth,)),
        ],
        compiler_params=pltpu.CompilerParams(
            collective_id=0, has_side_effects=True, vmem_limit_bytes=limit
        ),
        name="layers",
    )(blocks, dest, resets, w_query, gain, decay, cot)


def local(blocks, dest, resets, w_query, gain, decay, cot):
    groups = lax.axis_size("dp")
    segments = lax.axis_size("pipe")
    if segments == 2 and blocks.shape[0] == segments and groups == 16:
        return split_batches(blocks, dest, resets, w_query, gain, decay, cot)
    return pipelined(blocks, dest, resets, w_query, gain, decay, cot)


def solution(mesh):
    placed = (
        P(None, "dp", None),
        P(),
        P(),
        P("pipe", None, None),
        P("pipe", None),
        P("pipe", None),
        P(None, "dp", None),
    )
    return jax.shard_map(
        local, mesh=mesh, in_specs=placed, out_specs=P("pipe", "dp", None), check_vma=False
    )
```

```python
import functools

import jax
import jax.numpy as jnp
from jax import lax
from jax.experimental import pallas as pl
from jax.experimental.pallas import tpu as pltpu
from jax.sharding import PartitionSpec as P

CH = 4


EPS = 1e-05


def shifted(x, axis, by):
    devices = lax.axis_size(axis)
    pairs = [(i, i + by) for i in range(devices) if 0 <= i + by < devices]
    return lax.ppermute(x, axis, pairs)


def shortened(x):

    def short(part):
        return part.astype(jnp.bfloat16) if part.dtype == jnp.float32 else part

    return jax.tree.map(short, x)


def normed_project(x, weight, gain, extra):
    x32 = x.astype(jnp.float32)
    scale = lax.rsqrt(jnp.mean(x32 * x32, axis=-1, keepdims=True) + EPS)
    z = (x32 * scale * gain).astype(jnp.bfloat16)
    q = (jnp.dot(z, weight, preferred_element_type=jnp.float32) + extra).astype(jnp.bfloat16)
    return (z, q)


def tables(log_rate, flags):
    count = jnp.cumsum(flags)
    index = jnp.arange(flags.shape[0]).astype(jnp.float32)
    diff = index[:, None] - index[None, :]
    same = (count[:, None] == count[None, :]) & (diff >= 0)
    return jnp.where(same[None], jnp.exp(diff[None] * log_rate[:, None, None]), 0.0)


def section_tables(log_rate, flags):
    length = flags.shape[0]
    intra = tables(log_rate.reshape(-1), flags)
    return intra.reshape(log_rate.shape[0], log_rate.shape[1], length, length)


def finish(x, heads_out):
    normal = heads_out * lax.rsqrt(jnp.mean(heads_out * heads_out, axis=-1, keepdims=True) + EPS)
    return (x.astype(jnp.float32) + normal.reshape(x.shape)).astype(jnp.bfloat16)


def local_layer(x, extra, weight, gain_row, intra):
    z, q = normed_project(x, weight, gain_row, extra)
    heads = intra.shape[0]
    length = x.shape[0]
    query_rows = q.astype(jnp.float32).reshape(length, heads, -1)
    value_rows = z.reshape(length, heads, -1)
    scores = jnp.einsum("thk,shk->hts", query_rows, query_rows) * intra
    mixing_weights = scores.astype(jnp.bfloat16)
    outputs = jnp.einsum(
        "hts,shv->thv", mixing_weights, value_rows, preferred_element_type=jnp.float32
    )
    return (finish(x, outputs), z)


def section(x, extras, weight, gain, intra):
    normals = []
    for depth in range(weight.shape[0]):
        x, z = local_layer(x, extras[depth], weight[depth], gain[depth], intra[depth])
        normals.append(z)
    return (x, jnp.stack(normals))


def pipelined(blocks, dest, resets, w_query, gain, decay, cot):
    groups = lax.axis_size("dp")
    segments = lax.axis_size("pipe")
    rank = lax.axis_index("dp")
    segment = lax.axis_index("pipe")
    batches, rows, width = blocks.shape
    per_rank = rows // CH
    room = (per_rank + groups - 1) // groups
    mine = blocks.reshape(batches, per_rank, CH * width)
    own = lax.dynamic_index_in_dim(dest, rank, 1, keepdims=False)
    order = jnp.arange(per_rank)
    before_mask = order[None, :] < order[:, None]
    matching = own[:, :, None] == own[:, None, :]
    before = jnp.sum((matching & before_mask[None]).astype(jnp.int32), axis=2)
    target = own * room + before
    slot_ids = jnp.arange(groups * room, dtype=jnp.int32)
    send_map = (target[:, None, :] == slot_ids[None, :, None]).astype(jnp.bfloat16)
    outgoing = jnp.einsum(
        "mtj,mjc->mtc", send_map, mine, preferred_element_type=jnp.float32
    ).astype(jnp.bfloat16)
    incoming = lax.all_to_all(outgoing, "dp", split_axis=1, concat_axis=1, tiled=True)
    hits = (dest == rank).astype(jnp.int32)
    rank_in = jnp.cumsum(hits, axis=2) - 1
    senders = jnp.arange(groups, dtype=jnp.int32)[None, :, None]
    source = jnp.sum(hits * (senders * room + rank_in), axis=1)
    recv_map = (source[:, :, None] == slot_ids[None, None, :]).astype(jnp.bfloat16)
    packed = (
        jnp.einsum("mjt,mtc->mjc", recv_map, incoming, preferred_element_type=jnp.float32)
        .astype(jnp.bfloat16)
        .reshape(batches, rows, width)
    )
    positions = rank * rows + jnp.arange(rows, dtype=jnp.int32)
    flags = jnp.any(positions[None, :, None] == resets[:, None, :], axis=-1).astype(jnp.float32)
    layers = w_query.shape[0]
    hidden_qk = w_query.shape[2]
    log_rate = jnp.log(decay)
    zero_extra = jnp.zeros((layers, rows, hidden_qk), jnp.float32)
    zero_rows = jnp.zeros((rows, width), jnp.bfloat16)
    ticks = batches + segments - 1

    def forward_tick(tick, carry):
        inbox, saved_x = carry
        batch = tick - segment
        valid = (batch >= 0) & (batch < batches)
        pick = jnp.clip(batch, 0, batches - 1)
        x_in = jnp.where(
            segment == 0, lax.dynamic_index_in_dim(packed, pick, 0, keepdims=False), inbox
        )
        flag_row = lax.dynamic_index_in_dim(flags, pick, 0, keepdims=False)

        def forward_active(x):
            intra = section_tables(log_rate, flag_row)
            return section(x, zero_extra, w_query, gain, intra)[0]

        def forward_resting(x):
            return zero_rows

        output = lax.cond(valid, forward_active, forward_resting, x_in)
        keep_x = jnp.where(valid, x_in, lax.dynamic_index_in_dim(saved_x, pick, 0, keepdims=False))
        saved_x = lax.dynamic_update_index_in_dim(saved_x, keep_x, pick, 0)
        inbox = shifted(output, "pipe", 1)
        return (inbox, saved_x)

    start = (zero_rows, jnp.zeros((batches, rows, width), jnp.bfloat16))
    _, saved_x = lax.fori_loop(0, ticks, forward_tick, start)

    def backward_tick(tick, carry):
        inbox, grad_total = carry
        batch = tick - (segments - 1 - segment)
        valid = (batch >= 0) & (batch < batches)
        pick = jnp.clip(batch, 0, batches - 1)
        upstream = jnp.where(
            segment == segments - 1, lax.dynamic_index_in_dim(cot, pick, 0, keepdims=False), inbox
        )
        x_in = lax.dynamic_index_in_dim(saved_x, pick, 0, keepdims=False)
        flag_row = lax.dynamic_index_in_dim(flags, pick, 0, keepdims=False)

        def backward_active(args):
            x, d_out = args
            intra = section_tables(log_rate, flag_row)

            def mixing(x_arg, e_arg):
                return section(x_arg, e_arg, w_query, gain, intra)

            _, pullback, normal_rows = jax.vjp(mixing, x, zero_extra, has_aux=True)
            d_input, d_extra = pullback(d_out)
            d_weight = jnp.einsum(
                "ltd,ltk->ldk",
                normal_rows,
                d_extra.astype(jnp.bfloat16),
                preferred_element_type=jnp.float32,
            )
            return (d_input, d_weight)

        def backward_resting(args):
            return (zero_rows, jnp.zeros((layers, width, hidden_qk), jnp.float32))

        d_x, d_weight = lax.cond(valid, backward_active, backward_resting, (x_in, upstream))
        inbox = jax.tree.map(
            lambda part, own: part.astype(own.dtype), shifted(shortened(d_x), "pipe", -1), d_x
        )
        return (inbox, grad_total + d_weight)

    grad_start = (zero_rows, jnp.zeros((layers, width, hidden_qk), jnp.float32))
    _, grad_total = lax.fori_loop(0, ticks, backward_tick, grad_start)
    full = lax.psum(grad_total, "dp")
    share = width // groups
    own_rows = lax.dynamic_slice_in_dim(full, rank * share, share, 1)
    return own_rows


MESH = pl.DeviceIdType.MESH
F32 = jnp.float32
BF16 = jnp.bfloat16


def dot(a, b, ca=1, cb=0):
    return lax.dot_general(a, b, (((ca,), (cb,)), ((), ())), preferred_element_type=F32)


def iota(shape, dim):
    return lax.broadcasted_iota(jnp.int32, shape, dim)


def as_column(row):
    n = row.shape[1]
    eye = iota((n, n), 0) == iota((n, n), 1)
    return jnp.sum(jnp.where(eye, jnp.broadcast_to(row, (n, n)), 0), axis=1, keepdims=True)


SPLIT = 4


def begin_exchange(
    groups, slot, blocks_ref, dest_ref, w_ref, gain_ref, decay_ref,
    recv_ref, w_all, gain_all, decay_all,
    in_s, dest_s, out_s, in_sem, send_sem, recv_sem, par_send, par_recv, own_sem,
):
    me = lax.axis_index("dp")
    core = lax.axis_index("pipe")
    barrier = pltpu.get_barrier_semaphore()
    loads = [
        pltpu.make_async_copy(dest_ref.at[core], dest_s, in_sem.at[0]),
        pltpu.make_async_copy(blocks_ref.at[core], in_s, in_sem.at[1]),
    ]
    for load in loads:
        load.start()

    def greet(k, carry):
        pl.semaphore_signal(
            barrier, inc=1, device_id=(lax.rem(me + k, groups), core), device_id_type=MESH
        )
        return carry

    lax.fori_loop(1, groups, greet, 0)
    pl.semaphore_signal(barrier, inc=1, device_id=(me, 1 - core), device_id_type=MESH)

    own_copies = []
    for i, (src, dst) in enumerate(((w_ref, w_all), (gain_ref, gain_all), (decay_ref, decay_all))):
        own = pltpu.make_async_copy(src, dst.at[core], own_sem.at[i])
        own.start()
        own_copies.append(own)

    rows = blocks_ref.shape[1]
    per_rank = rows // CH
    total = groups * slot
    loads[0].wait()
    own_row = dest_s[pl.ds(me, 1), :]
    own_col = as_column(own_row)
    order = (per_rank, per_rank)
    earlier = (own_row == own_col) & (iota(order, 1) < iota(order, 0))
    before = jnp.sum(jnp.where(earlier, 1, 0), axis=1, keepdims=True)
    target = own_col * slot + before * CH
    wide = (per_rank, rows)
    spread = iota(wide, 1) // CH == iota(wide, 0)
    target_row = jnp.sum(jnp.where(spread, jnp.broadcast_to(target, wide), 0), axis=0, keepdims=True)
    target_row = target_row + iota((1, rows), 1) % CH
    loads[1].wait()
    lanes = in_s.shape[1] // SPLIT
    picked = jnp.zeros((total, lanes), F32)
    for c in range(SPLIT):
        wanted = target_row + c * (slot // SPLIT)
        send_map = jnp.where(iota((total, rows), 0) == wanted, 1.0, 0.0).astype(BF16)
        picked = picked + dot(send_map, in_s[:, c * lanes : (c + 1) * lanes])
    out_s[...] = picked.astype(BF16).reshape(out_s.shape)

    pl.semaphore_wait(barrier, groups)

    def pair_copy(k):
        there = lax.rem(me + k, groups)
        return pltpu.make_async_remote_copy(
            src_ref=out_s.at[there], dst_ref=recv_ref.at[me],
            send_sem=send_sem.at[k], recv_sem=recv_sem.at[k],
            device_id=(there, core), device_id_type=MESH,
        )

    def send(k, carry):
        pair_copy(k).start()
        return carry

    lax.fori_loop(1, groups, send, 0)
    part_copies = []
    for i, (src, dst) in enumerate(((w_ref, w_all), (gain_ref, gain_all), (decay_ref, decay_all))):
        part = pltpu.make_async_remote_copy(
            src_ref=src, dst_ref=dst.at[core], send_sem=par_send.at[i], recv_sem=par_recv.at[i],
            device_id=(me, 1 - core), device_id_type=MESH,
        )
        part.start()
        part_copies.append(part)
    recv_ref[me] = out_s[me]

    def scalars_here():
        own_copies[2].wait()
        part_copies[2].wait()

    def rest_here():
        for copy in own_copies[:2] + part_copies[:2]:
            copy.wait()

        def arrive(k, carry):
            pair_copy(k).wait()
            return carry

        lax.fori_loop(1, groups, arrive, 0)

    return scalars_here, rest_here


def layers_kernel(
    heads, slot, blocks_ref, dest_ref, resets_ref, w_own, gain_own, decay_own, cot_ref, out_ref,
    recv_ref, w_ref, gain_ref, decay_ref, blocks_s, out_s,
    blocks_sem, send_sem, recv_sem, par_send, par_recv, own_sem,
    dest_s, resets_s, z_s, g_s, q_s, x_s, a_s, table_s, n_s, ro_s, r_s, dy_s, dv_s,
    zr_s, gr_s, part_s, r1_s, h_s, r2_s, k_s, r3_s, fin_s, finr_s,
    in_sem, z_send, z_recv, g_send, g_recv, s1_send, s1_recv, s2_send, s2_recv,
    s3_send, s3_recv, f_send, f_recv,
):
    me = lax.axis_index("dp")
    core = lax.axis_index("pipe")
    layers, rows, width = z_s.shape
    depth, share, hidden = out_ref.shape
    half = hidden // 2
    nz = k_s.shape[1]
    dk = hidden // heads
    dv = width // heads
    per_rank = rows // CH
    groups = dest_ref.shape[1]
    x = me % 2
    y = (me // 2) % 2
    z_at = me // 4
    x_mate = me + 1 - 2 * x
    y_mate = me + 2 * (1 - 2 * y)
    peer = (me, 1 - core)
    loads = [
        pltpu.make_async_copy(resets_ref, resets_s, in_sem.at[0]),
        pltpu.make_async_copy(cot_ref.at[core], dy_s, in_sem.at[1]),
    ]
    for load in loads:
        load.start()
    scalars_here, rest_here = begin_exchange(
        groups, slot, blocks_ref, dest_ref, w_own, gain_own, decay_own,
        recv_ref, w_ref, gain_ref, decay_ref, blocks_s, dest_s, out_s,
        blocks_sem, send_sem, recv_sem, par_send, par_recv, own_sem,
    )

    def remote(src, dst, send, recv, mate):
        return pltpu.make_async_remote_copy(
            src_ref=src, dst_ref=dst, send_sem=send, recv_sem=recv,
            device_id=mate, device_id_type=MESH,
        )

    def z_copy(l):
        return remote(z_s.at[l], zr_s.at[l], z_send.at[l], z_recv.at[l], peer)

    hits = jnp.where(dest_s[...] == me, 1.0, 0.0)
    order = (per_rank, per_rank)
    upper = jnp.where(iota(order, 0) < iota(order, 1), 1.0, 0.0).astype(BF16)
    before = dot(hits.astype(BF16), upper)
    sender = iota((groups, per_rank), 0).astype(F32)
    source = jnp.sum(hits * (sender * slot + before * CH), axis=0, keepdims=True)
    tall = (rows, per_rank)
    spread = iota(tall, 0) // CH == iota(tall, 1)
    source_col = jnp.sum(jnp.where(spread, jnp.broadcast_to(source, tall), 0.0), axis=1, keepdims=True)
    source_col = source_col.astype(jnp.int32) + iota((rows, 1), 0) % CH
    loads[0].wait()
    resets = resets_s[pl.ds(core, 1), :]
    n_resets = resets.shape[1]
    start = me * rows
    count_col = jnp.sum(
        jnp.where(resets <= iota((rows, n_resets), 0) + start, 1, 0), axis=1, keepdims=True
    )
    count_row = jnp.sum(
        jnp.where(as_column(resets) <= iota((n_resets, rows), 1) + start, 1, 0), axis=0, keepdims=True
    )
    square = (rows, rows)
    steps = iota(square, 0) - iota(square, 1)
    same = (count_col == count_row) & (steps >= 0)
    diff = steps.astype(F32)

    scalars_here()

    def fill(l, carry):
        rates = jnp.log(decay_ref[l // depth, pl.ds(l % depth, 1), :])
        for h in range(heads):
            table_s[l, h] = jnp.where(same, jnp.exp(diff * rates[:, h : h + 1]), 0.0)
        return carry

    lax.fori_loop(0, layers, fill, 0)
    rest_here()
    lanes = width // SPLIT
    arrived = recv_ref[...].reshape(groups * slot, lanes)
    for c in range(SPLIT):
        wanted = source_col + c * (slot // SPLIT)
        recv_map = jnp.where(iota((rows, groups * slot), 1) == wanted, 1.0, 0.0).astype(BF16)
        x_s[0, :, c * lanes : (c + 1) * lanes] = dot(recv_map, arrived).astype(BF16)

    def forward(l, carry):
        x32 = x_s[l].astype(F32)
        scale = lax.rsqrt(jnp.mean(x32 * x32, axis=1, keepdims=True) + EPS)
        r_s[l] = scale
        gain = gain_ref[l // depth, pl.ds(l % depth, 1), :]
        z = (x32 * scale * gain).astype(BF16)
        z_s[l] = z
        z_copy(l).start()
        q = dot(z, w_ref[l // depth, l % depth]).astype(BF16)
        q_s[l] = q
        for h in range(heads):
            table = table_s[l, h]
            qh = q[:, h * dk : (h + 1) * dk]
            a = (dot(qh, qh, 1, 1) * table).astype(BF16)
            a_s[l, h] = a
            cols = slice(h * dv, (h + 1) * dv)
            o = dot(a, z[:, cols])
            ro = lax.rsqrt(jnp.mean(o * o, axis=1, keepdims=True) + EPS)
            n = o * ro
            n_s[l, :, cols] = n
            ro_s[l, h] = ro
            x_s[l + 1, :, cols] = (x32[:, cols] + n).astype(BF16)
        return carry

    lax.fori_loop(0, layers, forward, 0)
    loads[1].wait()
    copies = {}

    def begin(name, copy):
        copy.start()
        copies[name] = copy

    def places(l):
        by_x = (core + l) % 2
        by_y = 1 - by_x
        first = (by_x * x_mate + by_y * y_mate, core)
        second = (by_x * y_mate + by_y * x_mate, core)
        return by_x, by_y, by_x * x + by_y * y, by_x * y + by_y * x, first, second

    def weight_part(l):
        by_x, by_y, f, s, first, second = places(l)
        part = dot(z_s[l], g_s[l, core], 0, 0)
        copies["g", l].wait_recv()
        z_copy(l).wait_recv()
        part = part + dot(zr_s[l], gr_s[l], 0, 0)
        for d in range(groups):
            zd, yd, xd = d // 4, (d // 2) % 2, d % 2
            rows_d = part[d * share : (d + 1) * share].astype(BF16)
            part_s[l, by_x * xd + by_y * yd, by_x * yd + by_y * xd, zd] = rows_d
        begin(("s1", l), remote(part_s.at[l, 1 - f], r1_s.at[l], s1_send.at[l], s1_recv.at[l], first))

    def stage_two(l):
        _, _, f, s, first, second = places(l)
        copies["s1", l].wait_recv()
        total = part_s[l, f, 1 - s].astype(F32) + r1_s[l, 1 - s].astype(F32)
        h_s[l] = total.astype(BF16)
        begin(("s2", l), remote(h_s.at[l], r2_s.at[l], s2_send.at[l], s2_recv.at[l], second))

    def stage_three(l):
        _, _, f, s, first, second = places(l)
        copies["s2", l].wait_recv()
        total = part_s[l, f, s].astype(F32) + r1_s[l, s].astype(F32) + r2_s[l].astype(F32)
        k_s[l] = total.astype(BF16)
        for k in range(1, nz):
            there = (z_at + k) % nz
            begin(("s3", l, k), remote(
                k_s.at[l, there], r3_s.at[l, k - 1], s3_send.at[l, k - 1], s3_recv.at[l, k - 1],
                (there * 4 + me % 4, core),
            ))

    def finish_sum(l):
        total = k_s[l, z_at].astype(F32)
        for k in range(1, nz):
            copies["s3", l, k].wait_recv()
            total = total + r3_s[l, k - 1].astype(F32)
        fin_s[l] = total

    def backward(l):
        for h in range(heads):
            cols = slice(h * dv, (h + 1) * dv)
            dn = dy_s[:, cols].astype(F32)
            n = n_s[l, :, cols]
            do = ro_s[l, h] * (dn - n * jnp.mean(dn * n, axis=1, keepdims=True))
            do = do.astype(BF16)
            da = dot(do, z_s[l, :, cols], 1, 1)
            ds = (da * table_s[l, h]).astype(BF16)
            if l > 0:
                dv_s[:, cols] = dot(a_s[l, h], do, 0, 0)
            qh = q_s[l, :, h * dk : (h + 1) * dk]
            at = h * dk % half
            g_s[l, h * dk // half, :, at : at + dk] = (dot(ds, qh) + dot(ds, qh, 0, 0)).astype(BF16)
        begin(("g", l), remote(g_s.at[l, 1 - core], gr_s.at[l], g_send.at[l], g_recv.at[l], peer))
        if l > 0:
            w = w_ref[l // depth, l % depth]
            dz = dot(g_s[l, 0], w[:, :half], 1, 1) + dot(g_s[l, 1], w[:, half:], 1, 1) + dv_s[...]
            gain = gain_ref[l // depth, pl.ds(l % depth, 1), :]
            scale = r_s[l]
            unit = x_s[l].astype(F32) * scale
            dzg = dz * gain
            dx = scale * (dzg - unit * jnp.mean(dzg * unit, axis=1, keepdims=True))
            dy_s[...] = (dy_s[...].astype(F32) + dx).astype(BF16)

    for step in range(layers + 4):
        l = layers - 1 - step
        if l >= 0:
            backward(l)
        if 0 <= l + 2 < layers:
            stage_three(l + 2)
        if 0 <= l + 1 < layers:
            stage_two(l + 1)
        if l >= 0:
            weight_part(l)
        if 0 <= l + 4 < layers:
            finish_sum(l + 4)

    for s in range(depth):
        theirs = (1 - core) * depth + s
        begin(("f", s), remote(fin_s.at[theirs], finr_s.at[s], f_send.at[s], f_recv.at[s], peer))
    mine = pl.ds(pl.multiple_of(core * half, half), half)
    other = pl.ds(pl.multiple_of((1 - core) * half, half), half)
    for s in range(depth):
        out_ref[s, :, mine] = fin_s[core * depth + s]
    for s in range(depth):
        copies["f", s].wait_recv()
        out_ref[s, :, other] = finr_s[s]
    for copy in copies.values():
        copy.wait_send()
    for l in range(layers):
        z_copy(l).wait_send()


def split_batches(blocks, dest, resets, w_query, gain, decay, cot):
    groups = lax.axis_size("dp")
    segments = lax.axis_size("pipe")
    _, rows, width = blocks.shape
    depth, _, hidden = w_query.shape
    heads = decay.shape[1]
    layers = depth * segments
    room = (rows // CH + groups - 1) // groups
    slot = room * CH * SPLIT
    vmem = pl.BlockSpec(memory_space=pltpu.VMEM)
    hbm = pl.BlockSpec(memory_space=pltpu.HBM)
    dma = pltpu.SemaphoreType.DMA
    limit = 63 * 2**20
    share = width // groups
    nz = groups // 4
    half = hidden // 2
    return pl.pallas_call(
        functools.partial(layers_kernel, heads, slot),
        out_shape=jax.ShapeDtypeStruct((depth, share, hidden), F32),
        in_specs=[hbm] * 7,
        out_specs=vmem,
        scratch_shapes=[
            pltpu.VMEM((groups, slot, width // SPLIT), BF16),
            pltpu.VMEM((segments,) + w_query.shape, BF16),
            pltpu.VMEM((segments,) + gain.shape, F32),
            pltpu.VMEM((segments,) + decay.shape, F32),
            pltpu.VMEM((rows, width), BF16),
            pltpu.VMEM((groups, slot, width // SPLIT), BF16),
            dma((2,)), dma((groups,)), dma((groups,)), dma((3,)), dma((3,)), dma((3,)),
            pltpu.VMEM(dest.shape[1:], jnp.int32),
            pltpu.VMEM(resets.shape, jnp.int32),
            pltpu.VMEM((layers, rows, width), BF16),
            pltpu.VMEM((layers, 2, rows, half), BF16),
            pltpu.VMEM((layers, rows, hidden), BF16),
            pltpu.VMEM((layers + 1, rows, width), BF16),
            pltpu.VMEM((layers, heads, rows, rows), BF16),
            pltpu.VMEM((layers, heads, rows, rows), F32),
            pltpu.VMEM((layers, rows, width), F32),
            pltpu.VMEM((layers, heads, rows, 1), F32),
            pltpu.VMEM((layers, rows, 1), F32),
            pltpu.VMEM((rows, width), BF16),
            pltpu.VMEM((rows, width), F32),
            pltpu.VMEM((layers, rows, width), BF16),
            pltpu.VMEM((layers, rows, half), BF16),
            pltpu.VMEM((layers, 2, 2, nz, share, half), BF16),
            pltpu.VMEM((layers, 2, nz, share, half), BF16),
            pltpu.VMEM((layers, nz, share, half), BF16),
            pltpu.VMEM((layers, nz, share, half), BF16),
            pltpu.VMEM((layers, nz, share, half), BF16),
            pltpu.VMEM((layers, nz - 1, share, half), BF16),
            pltpu.VMEM((layers, share, half), F32),
            pltpu.VMEM((depth, share, half), F32),
            dma((2,)), dma((layers,)), dma((layers,)), dma((layers,)), dma((layers,)),
            dma((layers,)), dma((layers,)), dma((layers,)), dma((layers,)),
            dma((layers, nz - 1)), dma((layers, nz - 1)), dma((depth,)), dma((depth,)),
        ],
        compiler_params=pltpu.CompilerParams(
            collective_id=0, has_side_effects=True, vmem_limit_bytes=limit
        ),
        name="layers",
    )(blocks, dest, resets, w_query, gain, decay, cot)


def local(blocks, dest, resets, w_query, gain, decay, cot):
    groups = lax.axis_size("dp")
    segments = lax.axis_size("pipe")
    if segments == 2 and blocks.shape[0] == segments and groups == 16:
        return split_batches(blocks, dest, resets, w_query, gain, decay, cot)
    return pipelined(blocks, dest, resets, w_query, gain, decay, cot)


def solution(mesh):
    placed = (
        P(None, "dp", None),
        P(),
        P(),
        P("pipe", None, None),
        P("pipe", None),
        P("pipe", None),
        P(None, "dp", None),
    )
    return jax.shard_map(
        local, mesh=mesh, in_specs=placed, out_specs=P("pipe", "dp", None), check_vma=False
    )
```
